32 devices in a mesh: rows: 8 (over z, x), cols: 4 (over y, core).
Axes of the slice: x: 2, y: 2, z: 4, core: 2. Of those that a mesh axis runs over, the one named last changes fastest.
Arguments:
- vectors: bfloat16 [32768, 1024], P('rows'), may hold values from -6 to 6
- near_tiles: bfloat16 [128, 16, 256, 256], P(('rows', 'cols')), may hold values from -0.09375 to 0.09375
- near_cols: int32 [128, 16], P(('rows', 'cols')), may hold values from 0 to 19, as said below
- left_one: bfloat16 [32768, 512], P('rows', 'cols'), may hold values from -0.25 to 0.25
- right_one: bfloat16 [32768, 512], P('rows', 'cols'), may hold values from -0.046875 to 0.046875
- left_two: bfloat16 [32768, 512], P('rows', 'cols'), may hold values from -0.25 to 0.25
- right_two: bfloat16 [32768, 512], P('rows', 'cols'), may hold values from -0.0625 to 0.0625
Outputs:
- product: bfloat16 [32768, 1024], P(('rows', 'cols'))
The draws below stay inside these ranges and needn't reach their ends.
Inputs may be any that keep to these rules, and one draw needn't show every extreme that they name: `near_cols`: each row names 16 different column tiles of its window of 20.
All inputs are finite; a program needn't handle non-finite values.
Results may differ from the reference program's by a relative error of at most 0.014.
Values may be sent and summed in bfloat16 or wider, within the bound.
No kernel may reach another device: no remote copies, remote signals or barrier semaphores. Data moves between devices by JAX's collectives and lax.ppermute only.
A program may use at most 192 MiB of HBM per device.

```python
import jax
import jax.numpy as jnp
from jax import lax

B = 256
R = 512
NRHS = 1024
TILES_DEV = 16
NNZ = 16
REACH = 2
WINDOW = 20
NT = 128
NR = 32768
N_ROWS = 8


def draw_near_cols(key, part):
    scores = jax.random.randint(key, (NT, WINDOW), 0, 1 << 30)
    ranking = jnp.argsort(scores, axis=1, stable=True)
    return ranking[:, :NNZ].astype(jnp.int32)


def levels(stream_key, dims, cuts, low, top_value):
    loudness, own = 1.0, jax.random.fold_in(stream_key, 6)
    for position, parts in cuts:
        steps = jnp.exp(jax.random.uniform(jax.random.fold_in(own, position), (parts,), jnp.float32, low / len(cuts), top_value / len(cuts)))
        loudness = loudness * jnp.repeat(steps, dims[position] // parts).reshape([-1 if axis == position else 1 for axis in range(len(dims))])
    return loudness


def gaussian(own_key, shape, width, most, pieces=(), kind=jnp.bfloat16):
    array = jax.random.normal(own_key, shape, jnp.float32) * width
    if len(pieces) > 0:
        array = levels(own_key, shape, pieces, -0.22, 0.18) * array
    return jnp.clip(array, min=-most, max=most).astype(kind)


def setup_inputs(seed: int = 0) -> dict:
    key_list = jax.random.split(jax.random.key(seed), 8)
    return {
        "vectors": gaussian(key_list[0], (NR, NRHS), 1.0, 6.0, ((0, 8),)),
        "near_tiles": gaussian(key_list[1], (NT, NNZ, B, B), (NNZ * B) ** -0.5, 0.09375, ((0, 32),)),
        "near_cols": draw_near_cols(jax.random.fold_in(key_list[7], 71), 0),
        "left_one": gaussian(key_list[3], (NR, R), R ** -0.5, 0.25, ((0, 8), (1, 4))),
        "right_one": gaussian(key_list[4], (NR, R), (NR // 2) ** -0.5, 0.046875, ((0, 8), (1, 4))),
        "left_two": gaussian(key_list[5], (NR, R), R ** -0.5, 0.25, ((0, 8), (1, 4))),
        "right_two": gaussian(key_list[6], (NR, R), (NR // 4) ** -0.5, 0.0625, ((0, 8), (1, 4))),
    }


def near_range(padded, near_tiles, near_cols, range_index):
    begin = (range_index * TILES_DEV * B).astype(jnp.int32)
    window_rows = lax.dynamic_slice_in_dim(padded, begin, WINDOW * B, 0)
    blocks = window_rows.reshape(WINDOW, B, NRHS)
    leading_tile = (range_index * TILES_DEV).astype(jnp.int32)
    tiles_here = lax.dynamic_slice_in_dim(near_tiles, leading_tile, TILES_DEV, 0).astype(jnp.float32)
    cols_here = lax.dynamic_slice_in_dim(near_cols, leading_tile, TILES_DEV, 0)
    picked = blocks[cols_here]
    result = jnp.einsum("tkab,tkbn->tan", tiles_here, picked, precision=lax.Precision.HIGHEST)
    return result.reshape(TILES_DEV * B, NRHS)


def coupling(vectors_wide, left, right, groups):
    group_rows = NR // groups
    right_vector_sets = right.astype(jnp.float32).reshape(groups, group_rows, R)
    vector_sets = vectors_wide.reshape(groups, group_rows, NRHS)
    running_sums = jnp.einsum("qwh,qwp->qhp", right_vector_sets, vector_sets, precision=lax.Precision.HIGHEST)
    partner_index = running_sums.reshape(groups // 2, 2, R, NRHS)[:, ::-1].reshape(groups, R, NRHS)
    partner_index = lax.optimization_barrier(partner_index.astype(jnp.bfloat16)).astype(jnp.float32)
    left_vector_sets = left.astype(jnp.float32).reshape(groups, group_rows, R)
    coupled_result = jnp.einsum("dzl,dlk->dzk", left_vector_sets, partner_index, precision=lax.Precision.HIGHEST)
    return coupled_result.reshape(NR, NRHS)


def reference(vectors, near_tiles, near_cols, left_one, right_one, left_two, right_two):
    vectors_wide = vectors.astype(jnp.float32)
    padded = jnp.pad(vectors_wide, ((REACH * B, REACH * B), (0, 0)))
    near = lax.map(lambda index: near_range(padded, near_tiles, near_cols, index), jnp.arange(N_ROWS, dtype=jnp.int32))
    near = near.reshape(NR, NRHS)
    total = near + coupling(vectors_wide, left_one, right_one, 2) + coupling(vectors_wide, left_two, right_two, 4)
    return total.astype(jnp.bfloat16)
```

```python
import jax
import jax.numpy as jnp
from jax import lax
from jax.experimental import pallas as pl
from jax.experimental.pallas import tpu as pltpu
from jax.sharding import PartitionSpec as P

B = 256
REACH = 2
AXES = ("rows", "cols")
VMEM = 56 * 1024 * 1024


def moved(value, target):
    n_rows, n_cols = lax.axis_size("rows"), lax.axis_size("cols")
    pairs = []
    for row in range(n_rows):
        for col in range(n_cols):
            other = target(row, col)
            if 0 <= other[0] < n_rows:
                pairs.append((row * n_cols + col, other[0] * n_cols + other[1]))
    return lax.ppermute(value, AXES, pairs)


def flipped(value, row_bits, col_bits):
    return moved(value, lambda row, col: (row ^ row_bits, col ^ col_bits))


def project(half, right_one, right_two, vectors):
    depth, rank = right_one.shape
    width = vectors.shape[1] // 2
    step = min(512, depth)
    steps = depth // step

    def kernel(half_ref, one_ref, two_ref, vectors_ref, out_ref, acc_ref):
        k = pl.program_id(0)
        both = jnp.concatenate([one_ref[...], two_ref[...]], axis=1)
        part = lax.dot_general(
            both, vectors_ref[...], (((0,), (0,)), ((), ())), preferred_element_type=jnp.float32
        )

        @pl.when(k == 0)
        def _():
            acc_ref[...] = part

        @pl.when(k > 0)
        def _():
            acc_ref[...] += part

        @pl.when(k == steps - 1)
        def _():
            out_ref[...] = acc_ref[...].astype(jnp.bfloat16)

    return pl.pallas_call(
        kernel,
        out_shape=jax.ShapeDtypeStruct((2 * rank, width), jnp.bfloat16),
        grid_spec=pltpu.PrefetchScalarGridSpec(
            num_scalar_prefetch=1,
            grid=(steps,),
            in_specs=[
                pl.BlockSpec((step, rank), lambda k, half: (k, 0)),
                pl.BlockSpec((step, rank), lambda k, half: (k, 0)),
                pl.BlockSpec((step, width), lambda k, half: (k, half[0])),
            ],
            out_specs=pl.BlockSpec((2 * rank, width), lambda k, half: (0, 0)),
            scratch_shapes=[pltpu.VMEM((2 * rank, width), jnp.float32)],
        ),
        compiler_params=pltpu.CompilerParams(vmem_limit_bytes=VMEM),
        cost_estimate=pl.CostEstimate(
            flops=4 * rank * width * depth, bytes_accessed=2 * depth * (2 * rank + width), transcendentals=0
        ),
        name="project",
    )(half, right_one, right_two, vectors)


def near_inside(slots, near_tiles, vectors, first, count):
    _, nnz, _, _ = near_tiles.shape
    depth, width = vectors.shape
    inside = depth // B

    def kernel(slots_ref, tiles_ref, vectors_ref, out_ref, row_ref):
        t = pl.program_id(0) + first
        for col in range(inside):
            slot = slots_ref[t, col + REACH]
            tile = tiles_ref[0, jnp.maximum(slot, 0)]
            row_ref[:, col * B : (col + 1) * B] = jnp.where(slot >= 0, tile, jnp.zeros_like(tile))
        out_ref[...] = jnp.dot(row_ref[...], vectors_ref[...], preferred_element_type=jnp.float32)

    return pl.pallas_call(
        kernel,
        out_shape=jax.ShapeDtypeStruct((count * B, width), jnp.float32),
        grid_spec=pltpu.PrefetchScalarGridSpec(
            num_scalar_prefetch=1,
            grid=(count,),
            in_specs=[
                pl.BlockSpec((1, nnz, B, B), lambda t, slots: (t + first, 0, 0, 0)),
                pl.BlockSpec((depth, width), lambda t, slots: (0, 0)),
            ],
            out_specs=pl.BlockSpec((B, width), lambda t, slots: (t, 0)),
            scratch_shapes=[pltpu.VMEM((B, depth), jnp.bfloat16)],
        ),
        compiler_params=pltpu.CompilerParams(vmem_limit_bytes=VMEM),
        cost_estimate=pl.CostEstimate(
            flops=2 * count * B * depth * width,
            bytes_accessed=count * nnz * B * B * 2 + depth * width * 2 + count * B * width * 4,
            transcendentals=0,
        ),
        name="near_inside",
    )(slots, near_tiles, vectors)


def finish(where, halo_slots, near, near_tiles, halos, left_own, left_other, coeffs):
    tiles = near_tiles.shape[0]
    rows, width = near.shape
    half_width = width // 2
    rank = left_own[0].shape[1]
    outside = halo_slots.shape[1]
    per_half = len(coeffs) // 2
    others = len(left_other)

    def kernel(where_ref, slots_ref, near_ref, *refs):
        tile_refs, refs = refs[:outside], refs[outside:]
        halo_refs, refs = refs[:2], refs[2:]
        own_refs, refs = refs[:2], refs[2:]
        other_refs, refs = refs[:others], refs[others:]
        mine_refs, theirs_refs, out_ref = refs[:per_half], refs[per_half : 2 * per_half], refs[-1]
        j, t = pl.program_id(0), pl.program_id(1)
        wide = []
        for i in range(outside):
            tile = tile_refs[i][0, 0]
            wide.append(jnp.where(slots_ref[t, i] >= 0, tile, jnp.zeros_like(tile)))
        for level in range(2):
            wide.append(own_refs[level][...])
            wide += [ref[level] for ref in other_refs]
        wide = jnp.concatenate(wide, axis=1)

        def put(coeff_refs):
            tall = [ref[...] for ref in halo_refs]
            for level in range(2):
                tall += [ref[level * rank : (level + 1) * rank] for ref in coeff_refs]
            tall = jnp.concatenate(tall, axis=0)
            out_ref[...] = (
                near_ref[...] + jnp.dot(wide, tall, preferred_element_type=jnp.float32)
            ).astype(jnp.bfloat16)

        pl.when(j == 0)(lambda: put(mine_refs))
        pl.when(j == 1)(lambda: put(theirs_refs))

    def tile_spec(i):
        return pl.BlockSpec(
            (1, 1, B, B), lambda j, t, where, slots: (t, jnp.maximum(slots[t, i], 0), 0, 0)
        )

    def by_half(j, where):
        return jnp.bitwise_xor(j, where[0])

    return pl.pallas_call(
        kernel,
        out_shape=jax.ShapeDtypeStruct((rows, width), jnp.bfloat16),
        grid_spec=pltpu.PrefetchScalarGridSpec(
            num_scalar_prefetch=2,
            grid=(2, tiles),
            in_specs=[pl.BlockSpec((B, half_width), lambda j, t, where, slots: (t, by_half(j, where)))]
            + [tile_spec(i) for i in range(outside)]
            + [
                pl.BlockSpec((REACH * B, half_width), lambda j, t, where, slots: (0, by_half(j, where)))
                for _ in range(2)
            ]
            + [
                pl.BlockSpec((B, rank), lambda j, t, where, slots: (where[1] * tiles + t, 0))
                for _ in range(2)
            ]
            + [pl.BlockSpec((2, B, rank), lambda j, t, where, slots: (0, t, 0)) for _ in range(others)]
            + [
                pl.BlockSpec((2 * rank, half_width), lambda j, t, where, slots: (0, 0))
                for _ in range(2 * per_half)
            ],
            out_specs=pl.BlockSpec((B, half_width), lambda j, t, where, slots: (t, by_half(j, where))),
        ),
        compiler_params=pltpu.CompilerParams(vmem_limit_bytes=VMEM),
        cost_estimate=pl.CostEstimate(
            flops=2 * rows * width * (outside * B + 2 * per_half * rank),
            bytes_accessed=rows * width * 6 + 16 * 2**20,
            transcendentals=0,
        ),
        name="finish",
    )(where, halo_slots, near, *([near_tiles] * outside), *halos, *left_own, *left_other, *coeffs)


def per_device(vectors, near_tiles, near_cols, left_one, right_one, left_two, right_two):
    n_rows, n_cols = lax.axis_size("rows"), lax.axis_size("cols")
    bits = n_rows.bit_length() - 1
    row, col = lax.axis_index("rows"), lax.axis_index("cols")
    half, core = row % 2, col % 2
    depth, width = vectors.shape
    rank = right_one.shape[1]
    inside = depth // B
    window = inside + 2 * REACH

    nnz = near_cols.shape[1]
    names = near_cols[:, :, None] == jnp.arange(window, dtype=jnp.int32)
    slots = jnp.max(jnp.where(names, jnp.arange(nnz, dtype=jnp.int32)[None, :, None], -1), axis=1)

    send = project((1 - half).reshape(1), right_one, right_two, vectors)
    arrived = flipped(send, 1, 0)
    keep = project(half.reshape(1), right_one, right_two, vectors)

    edge = lax.dynamic_slice_in_dim(
        vectors, jnp.where(core == 0, depth - REACH * B, 0), REACH * B, axis=0
    )
    halo_mine = moved(edge, lambda r, c: (r + 1 if c % 2 == 0 else r - 1, c))

    share = depth // n_cols
    left_other = []
    for offset in range(1, n_cols):
        begin = (col ^ offset) * share
        piece = jnp.stack(
            [lax.dynamic_slice_in_dim(left, begin, share, axis=0) for left in (left_one, left_two)]
        )
        left_other.append(flipped(piece, 0, offset))

    near = near_inside(slots, near_tiles, vectors, 0, near_tiles.shape[0])

    def summed(a, b):
        return (a.astype(jnp.float32) + b.astype(jnp.float32)).astype(jnp.bfloat16)

    both = summed(keep, arrived)
    for bit in range(1, bits - 2):
        both = summed(both, flipped(both, 2**bit, 0))
    arrived = flipped(both, 2 ** (bits - 2), 0)
    one = summed(both[:rank], arrived[:rank])
    one = flipped(one, 2 ** (bits - 1), 0)
    both = jnp.concatenate([one, arrived[rank:]], axis=0)

    coeffs = []
    for other in range(2):
        for offset in range(0, n_cols, 2):
            there = both if (other, offset) == (0, 0) else flipped(both, other, offset)
            coeffs += [there, flipped(there, 0, 1)]

    halo_other = flipped(halo_mine, 0, 1)
    before, after = slots[:, :REACH], slots[:, window - REACH :]
    halo_slots = jnp.where(
        core == 0,
        jnp.concatenate([before, after], axis=1),
        jnp.concatenate([after, before], axis=1),
    )
    return finish(
        jnp.stack([half, col]),
        halo_slots,
        near,
        near_tiles,
        (halo_mine, halo_other),
        (left_one, left_two),
        left_other,
        coeffs,
    )


def solution(mesh):
    placed = (
        P("rows", None),
        P(("rows", "cols"), None, None, None),
        P(("rows", "cols"), None),
        P("rows", "cols"),
        P("rows", "cols"),
        P("rows", "cols"),
        P("rows", "cols"),
    )
    return jax.shard_map(
        per_device, mesh=mesh, in_specs=placed, out_specs=P(("rows", "cols"), None), check_vma=False
    )
```

```python
import jax
import jax.numpy as jnp
from jax import lax
from jax.experimental import pallas as pl
from jax.experimental.pallas import tpu as pltpu
from jax.sharding import PartitionSpec as P

B = 256
REACH = 2
AXES = ("rows", "cols")
VMEM = 32 * 1024 * 1024
ANY = pl.BlockSpec(memory_space=pl.ANY)
SMEM = pl.BlockSpec(memory_space=pltpu.SMEM)


def moved(value, target):
    n_rows, n_cols = lax.axis_size("rows"), lax.axis_size("cols")
    pairs = []
    for row in range(n_rows):
        for col in range(n_cols):
            other = target(row, col)
            if 0 <= other[0] < n_rows:
                pairs.append((row * n_cols + col, other[0] * n_cols + other[1]))
    return lax.ppermute(value, AXES, pairs)


def flipped(value, row_bits, col_bits):
    return moved(value, lambda row, col: (row ^ row_bits, col ^ col_bits))


def span(index, size):
    return pl.ds(pl.multiple_of(index * size, size), size)


def called(kernel, name, smem, hbm, after, out_shape, scratch, flops, moved_bytes):
    return pl.pallas_call(
        kernel,
        out_shape=out_shape,
        in_specs=[SMEM] * len(smem) + [ANY] * (len(hbm) + len(after)),
        out_specs=jax.tree.map(lambda _: ANY, out_shape),
        scratch_shapes=scratch,
        compiler_params=pltpu.CompilerParams(vmem_limit_bytes=VMEM),
        cost_estimate=pl.CostEstimate(flops=flops, bytes_accessed=moved_bytes, transcendentals=0),
        name=name,
    )(*smem, *hbm, *after)


def project(where, right_one, right_two, vectors, other, with_edge, after=()):
    depth, rank = right_one.shape
    width = vectors.shape[1] // 2
    parts = 8
    step = depth // parts
    edge = REACH * B

    def kernel(where_ref, one_ref, two_ref, vectors_ref, *refs):
        refs = refs[len(after) :]
        outs, refs = refs[: 1 + with_edge], refs[1 + with_edge :]
        rights, block, total, result, right_sems, block_sems, out_sems = refs
        half = where_ref[0] ^ 1 if other else where_ref[0]
        copies = []
        for i in range(parts):
            rows = pl.ds(i * step, step)
            copies.append(
                [
                    pltpu.make_async_copy(
                        ref.at[rows], rights.at[rows, pl.ds(level * rank, rank)], right_sems.at[level, i]
                    )
                    for level, ref in enumerate((one_ref, two_ref))
                ]
                + [
                    pltpu.make_async_copy(
                        vectors_ref.at[rows, span(half, width)], block.at[rows], block_sems.at[i]
                    )
                ]
            )
            for copy in copies[-1]:
                copy.start()
        if with_edge:
            begin = pl.multiple_of(jnp.where(where_ref[1] % 2 == 0, depth - edge, 0), edge)
            edge_copy = pltpu.make_async_copy(vectors_ref.at[pl.ds(begin, edge)], outs[1], out_sems.at[1])
            edge_copy.start()
        for i in range(parts):
            for copy in copies[i]:
                copy.wait()
            rows = pl.ds(i * step, step)
            part = lax.dot_general(
                rights[rows], block[rows], (((0,), (0,)), ((), ())), preferred_element_type=jnp.float32
            )
            if i == 0:
                total[...] = part
            elif i < parts - 1:
                total[...] += part
            else:
                result[...] = (total[...] + part).astype(jnp.bfloat16)
        out_copy = pltpu.make_async_copy(result, outs[0], out_sems.at[0])
        out_copy.start()
        out_copy.wait()
        if with_edge:
            edge_copy.wait()

    out = [jax.ShapeDtypeStruct((2 * rank, width), jnp.bfloat16)]
    if with_edge:
        out.append(jax.ShapeDtypeStruct((edge, vectors.shape[1]), jnp.bfloat16))
    return called(
        kernel,
        "project",
        [where],
        [right_one, right_two, vectors],
        after,
        out,
        [
            pltpu.VMEM((depth, 2 * rank), jnp.bfloat16),
            pltpu.VMEM((depth, width), jnp.bfloat16),
            pltpu.VMEM((2 * rank, width), jnp.float32),
            pltpu.VMEM((2 * rank, width), jnp.bfloat16),
            pltpu.SemaphoreType.DMA((2, parts)),
            pltpu.SemaphoreType.DMA((parts,)),
            pltpu.SemaphoreType.DMA((2,)),
        ],
        4 * rank * width * depth,
        2 * depth * (2 * rank + width),
    )


def near_inside(slots, near_tiles, vectors, first, count, sofar, after=()):
    tiles = near_tiles.shape[0]
    rows, width = tiles * B, vectors.shape[1]
    group = min(2, count)
    groups = count // group
    half = width // 2
    given = 0 if sofar is None else 1

    def kernel(slots_ref, tiles_ref, vectors_ref, *refs):
        sofar_refs, refs = refs[:given], refs[given + len(after) :]
        out_ref, wide, tall, total, result, tile_sems, vector_sems, sofar_sem, out_sems = refs

        def tile_copy(t, c):
            slot = slots_ref[t, first + c + REACH]
            copy = pltpu.make_async_copy(
                tiles_ref.at[t, jnp.maximum(slot, 0)],
                wide.at[pl.ds(t * B, B), pl.ds(c * B, B)],
                tile_sems.at[t, c],
            )
            return slot >= 0, copy

        def vector_copy(c):
            return pltpu.make_async_copy(
                vectors_ref.at[pl.ds((first + c) * B, B)], tall.at[pl.ds(c * B, B)], vector_sems.at[c]
            )

        if given:
            sofar_copy = pltpu.make_async_copy(sofar_refs[0], result, sofar_sem)
        for c in range(count):
            vector_copy(c).start()
            for t in range(tiles):
                there, copy = tile_copy(t, c)
                pl.when(there)(copy.start)

                @pl.when(jnp.logical_not(there))
                def _():
                    wide[t * B : (t + 1) * B, c * B : (c + 1) * B] = jnp.zeros((B, B), jnp.bfloat16)

            if given and c == group - 1:
                sofar_copy.start()
        out_copies = []
        for g in range(groups):
            for c in range(g * group, (g + 1) * group):
                vector_copy(c).wait()
                for t in range(tiles):
                    there, copy = tile_copy(t, c)
                    pl.when(there)(copy.wait)
            chosen = pl.ds(g * group * B, group * B)
            if given and g == groups - 1:
                sofar_copy.wait()
            for n in range(2):
                columns = pl.ds(n * half, half)
                part = jnp.dot(wide[:, chosen], tall[chosen, columns], preferred_element_type=jnp.float32)
                if g > 0:
                    part = total[:, columns] + part
                if g < groups - 1:
                    total[:, columns] = part
                else:
                    if given:
                        part = part + result[:, columns].astype(jnp.float32)
                    result[:, columns] = part.astype(jnp.bfloat16)
                    out_copies.append(
                        pltpu.make_async_copy(result.at[:, columns], out_ref.at[:, columns], out_sems.at[n])
                    )
                    out_copies[-1].start()
        for copy in out_copies:
            copy.wait()

    return called(
        kernel,
        "near_inside",
        [slots],
        [near_tiles, vectors] + ([sofar] if given else []),
        after,
        jax.ShapeDtypeStruct((rows, width), jnp.bfloat16),
        [
            pltpu.VMEM((rows, count * B), jnp.bfloat16),
            pltpu.VMEM((count * B, width), jnp.bfloat16),
            pltpu.VMEM((rows, width), jnp.float32),
            pltpu.VMEM((rows, width), jnp.bfloat16),
            pltpu.SemaphoreType.DMA((tiles, count)),
            pltpu.SemaphoreType.DMA((count,)),
            pltpu.SemaphoreType.DMA,
            pltpu.SemaphoreType.DMA((2,)),
        ],
        2 * rows * count * B * width,
        2 * count * B * (rows + width) + 2 * rows * width,
    )


def add_level(where, slots, sofar, near_tiles, halos, level, left, left_other, coeffs, after=()):
    rows, width = sofar.shape
    tiles = rows // B
    half = width // 2
    rank = left.shape[1]
    outside = 2 * REACH if halos else 0
    window = slots.shape[1]
    others = len(left_other)
    offsets = others + 1
    depth = outside * B + offsets * rank

    def kernel(where_ref, slots_ref, sofar_ref, tiles_ref, left_ref, *refs):
        other_refs, refs = refs[:others], refs[others:]
        coeff_refs, refs = refs[: 2 * offsets], refs[2 * offsets :]
        halo_refs, refs = refs[: len(halos)], refs[len(halos) + len(after) :]
        out_ref, wide, tall, result, tile_sems, halo_sems, left_sems, coeff_sems, sofar_sem, out_sems = refs
        mine, core = where_ref[0], where_ref[1] % 2

        def tile_copy(t, i):
            before = (i < REACH) == (core == 0)
            slot = slots_ref[t, jnp.where(before, i % REACH, window - REACH + i % REACH)]
            copy = pltpu.make_async_copy(
                tiles_ref.at[t, jnp.maximum(slot, 0)],
                wide.at[pl.ds(t * B, B), pl.ds(i * B, B)],
                tile_sems.at[t, i],
            )
            return slot >= 0, copy

        copies = []
        for i in range(outside):
            for t in range(tiles):
                there, copy = tile_copy(t, i)
                pl.when(there)(copy.start)

                @pl.when(jnp.logical_not(there))
                def _():
                    wide[t * B : (t + 1) * B, i * B : (i + 1) * B] = jnp.zeros((B, B), jnp.bfloat16)

        for i in range(len(halos)):
            copies.append(
                pltpu.make_async_copy(
                    halo_refs[i], tall.at[pl.ds(i * REACH * B, REACH * B)], halo_sems.at[i]
                )
            )
        for d in range(offsets):
            source = left_ref.at[span(where_ref[1], rows)] if d == 0 else other_refs[d - 1].at[level]
            place = outside * B + d * rank
            copies.append(
                pltpu.make_async_copy(source, wide.at[:, pl.ds(place, rank)], left_sems.at[d])
            )
            for other in range(2):
                copies.append(
                    pltpu.make_async_copy(
                        coeff_refs[other * offsets + d],
                        tall.at[pl.ds(place, rank), span(mine ^ other, half)],
                        coeff_sems.at[other, d],
                    )
                )
        copies.append(pltpu.make_async_copy(sofar_ref, result, sofar_sem))
        for copy in copies:
            copy.start()
        for copy in copies:
            copy.wait()
        for i in range(outside):
            for t in range(tiles):
                there, copy = tile_copy(t, i)
                pl.when(there)(copy.wait)
        out_copies = []
        for n in range(2):
            columns = pl.ds(n * half, half)
            part = jnp.dot(wide[...], tall[:, columns], preferred_element_type=jnp.float32)
            result[:, columns] = (result[:, columns].astype(jnp.float32) + part).astype(jnp.bfloat16)
            out_copies.append(
                pltpu.make_async_copy(result.at[:, columns], out_ref.at[:, columns], out_sems.at[n])
            )
            out_copies[-1].start()
        for copy in out_copies:
            copy.wait()

    return called(
        kernel,
        "add_level",
        [where, slots],
        [sofar, near_tiles, left, *left_other, *coeffs, *halos],
        after,
        jax.ShapeDtypeStruct((rows, width), jnp.bfloat16),
        [
            pltpu.VMEM((rows, depth), jnp.bfloat16),
            pltpu.VMEM((depth, width), jnp.bfloat16),
            pltpu.VMEM((rows, width), jnp.bfloat16),
            pltpu.SemaphoreType.DMA((tiles, max(outside, 1))),
            pltpu.SemaphoreType.DMA((2,)),
            pltpu.SemaphoreType.DMA((offsets,)),
            pltpu.SemaphoreType.DMA((2, offsets)),
            pltpu.SemaphoreType.DMA,
            pltpu.SemaphoreType.DMA((2,)),
        ],
        2 * rows * depth * width,
        2 * depth * (rows + width) + 4 * rows * width,
    )


def per_device(vectors, near_tiles, near_cols, left_one, right_one, left_two, right_two):
    n_rows, n_cols = lax.axis_size("rows"), lax.axis_size("cols")
    bits = n_rows.bit_length() - 1
    row, col = lax.axis_index("rows"), lax.axis_index("cols")
    depth = vectors.shape[0]
    rank = right_one.shape[1]
    inside = depth // B
    where = jnp.stack([row % 2, col])

    (send,) = project(where, right_one, right_two, vectors, True, False)
    arrived = flipped(send, 1, 0)
    keep, edge = project(where, right_one, right_two, vectors, False, True, after=(send,))

    nnz = near_cols.shape[1]
    names = near_cols[:, :, None] == jnp.arange(inside + 2 * REACH, dtype=jnp.int32)
    slots = jnp.max(jnp.where(names, jnp.arange(nnz, dtype=jnp.int32)[None, :, None], -1), axis=1)

    share = depth // n_cols
    left_other = []
    for offset in range(1, n_cols):
        begin = (col ^ offset) * share
        piece = jnp.stack(
            [lax.dynamic_slice_in_dim(left, begin, share, axis=0) for left in (left_one, left_two)]
        )
        left_other.append(flipped(piece, 0, offset))

    def summed(a, b):
        return (a.astype(jnp.float32) + b.astype(jnp.float32)).astype(jnp.bfloat16)

    near = near_inside(slots, near_tiles, vectors, 0, inside // 2, None, after=(keep,))
    both = summed(keep, arrived)

    halo_mine = moved(edge, lambda r, c: (r + 1 if c % 2 == 0 else r - 1, c))

    for bit in range(1, bits - 2):
        both = summed(both, flipped(both, 2**bit, 0))
    arrived = flipped(both, 2 ** (bits - 2), 0)
    near = near_inside(slots, near_tiles, vectors, inside // 2, inside // 2, near, after=(both,))
    one = flipped(summed(both[:rank], arrived[:rank]), 2 ** (bits - 1), 0)
    two = arrived[rank:]

    def gathered(value):
        found = []
        for other in range(2):
            for offset in range(0, n_cols, 2):
                there = value if (other, offset) == (0, 0) else flipped(value, other, offset)
                found += [there, flipped(there, 0, 1)]
        return found

    coeffs_two = gathered(two)
    halos = (halo_mine, flipped(halo_mine, 0, 1))
    coeffs_one = gathered(one)
    near = add_level(where, slots, near, near_tiles, halos, 1, left_two, left_other, coeffs_two)
    return add_level(where, slots, near, near_tiles, (), 0, left_one, left_other, coeffs_one)


def solution(mesh):
    placed = (
        P("rows", None),
        P(("rows", "cols"), None, None, None),
        P(("rows", "cols"), None),
        P("rows", "cols"),
        P("rows", "cols"),
        P("rows", "cols"),
        P("rows", "cols"),
    )
    return jax.shard_map(
        per_device, mesh=mesh, in_specs=placed, out_specs=P(("rows", "cols"), None), check_vma=False
    )
```

```python
import jax
import jax.numpy as jnp
from jax import lax
from jax.experimental import pallas as pl
from jax.experimental.pallas import tpu as pltpu
from jax.sharding import PartitionSpec as P

B = 256
REACH = 2
AXES = ("rows", "cols")
VMEM = 64 * 1024 * 1024
COST_A = 1
COST_B = 10**10
COST_C = 1
HBM = pl.BlockSpec(memory_space=pltpu.HBM)
SMEM = pl.BlockSpec(memory_space=pltpu.SMEM)


def moved(value, target):
    n_rows, n_cols = lax.axis_size("rows"), lax.axis_size("cols")
    pairs = []
    for row in range(n_rows):
        for col in range(n_cols):
            other = target(row, col)
            if other is not None and 0 <= other[0] < n_rows:
                pairs.append((row * n_cols + col, other[0] * n_cols + other[1]))
    return lax.ppermute(value, AXES, pairs)


def flipped(value, row_bits, col_bits):
    return moved(value, lambda row, col: (row ^ row_bits, col ^ col_bits))


def span(index, size):
    return pl.ds(pl.multiple_of(index * size, size), size)


def called(kernel, name, smem, hbm, after, out_shape, scratch, aliases={}, flops=1):
    return pl.pallas_call(
        kernel,
        out_shape=out_shape,
        in_specs=[SMEM] * len(smem) + [HBM] * (len(hbm) + len(after)),
        out_specs=jax.tree.map(lambda _: HBM, out_shape),
        scratch_shapes=scratch,
        input_output_aliases=aliases,
        compiler_params=pltpu.CompilerParams(vmem_limit_bytes=VMEM),
        cost_estimate=pl.CostEstimate(flops=flops, bytes_accessed=1, transcendentals=0),
        name=name,
    )(*smem, *hbm, *after)


def project(right_one, right_two, vectors):
    depth, rank = right_one.shape
    width = vectors.shape[1]
    half = width // 2
    step = REACH * B
    parts = depth // step

    def kernel(one_ref, two_ref, vectors_ref, send_ref, keep_ref, token_ref, edge_ref, *scratch):
        rights, block, total, result, right_sems, block_sems, out_sems, edge_sems = scratch
        mine, last_first = lax.axis_index("rows") % 2, lax.axis_index("cols") % 2 == 0
        copies, places = [], []
        for i in range(parts):
            place = span(jnp.where(last_first, parts - 1 - i, i), step)
            places.append(place)
            copies.append(
                [
                    pltpu.make_async_copy(
                        ref.at[place], rights.at[place, pl.ds(level * rank, rank)], right_sems.at[level, i]
                    )
                    for level, ref in enumerate((one_ref, two_ref))
                ]
                + [pltpu.make_async_copy(vectors_ref.at[place], block.at[place], block_sems.at[i])]
            )
            for copy in copies[-1]:
                copy.start()
        edge_copy = pltpu.make_async_copy(block.at[places[0]], edge_ref, edge_sems.at[0])
        for i in range(parts):
            for copy in copies[i]:
                copy.wait()
            if i == 0:
                edge_copy.start()
            part = lax.dot_general(
                rights[places[i]], block[places[i]], (((0,), (0,)), ((), ())), preferred_element_type=jnp.float32
            )
            if i == 0:
                total[...] = part
            elif i < parts - 1:
                total[...] += part
            else:
                result[...] = (total[...] + part).astype(jnp.bfloat16)
        outs = [pltpu.make_async_copy(result.at[pl.ds(0, 16), pl.ds(0, 128)], token_ref, edge_sems.at[1])]
        for k, (ref, chosen) in enumerate(((send_ref, mine ^ 1), (keep_ref, mine))):
            outs.append(
                pltpu.make_async_copy(
                    result.at[pl.ds(0, rank), span(chosen, half)], ref.at[pl.ds(0, rank)], out_sems.at[k, 0]
                )
            )
            for n in range(2):
                outs.append(
                    pltpu.make_async_copy(
                        result.at[pl.ds(rank, rank), pl.ds(n * half, half)],
                        ref.at[pl.ds((1 + n) * rank, rank)],
                        out_sems.at[k, 1 + n],
                    )
                )
        for copy in outs:
            copy.start()
        for copy in outs:
            copy.wait()
        edge_copy.wait()

    return called(
        kernel,
        "project",
        [],
        [right_one, right_two, vectors],
        (),
        [
            jax.ShapeDtypeStruct((3 * rank, half), jnp.bfloat16),
            jax.ShapeDtypeStruct((3 * rank, half), jnp.bfloat16),
            jax.ShapeDtypeStruct((16, 128), jnp.bfloat16),
            jax.ShapeDtypeStruct((step, width), jnp.bfloat16),
        ],
        [
            pltpu.VMEM((depth, 2 * rank), jnp.bfloat16),
            pltpu.VMEM((depth, width), jnp.bfloat16),
            pltpu.VMEM((2 * rank, width), jnp.float32),
            pltpu.VMEM((2 * rank, width), jnp.bfloat16),
            pltpu.SemaphoreType.DMA((2, parts)),
            pltpu.SemaphoreType.DMA((parts,)),
            pltpu.SemaphoreType.DMA((2, 3)),
            pltpu.SemaphoreType.DMA((2,)),
        ],
    )


def near_inside(slots, near_tiles, vectors, first, count, sofar, lefts, flops, after=()):
    tiles = near_tiles.shape[0]
    rows, width = tiles * B, vectors.shape[1]
    group = 2
    groups = count // group
    half = width // 2
    given = 0 if sofar is None else 1
    shares = lefts[0].shape[0] // rows if lefts else 0
    more = 1 if lefts else 0
    rank = lefts[0].shape[1] if lefts else 0

    def kernel(slots_ref, tiles_ref, vectors_ref, *refs):
        sofar_refs, refs = refs[:given], refs[given:]
        left_refs, refs = refs[: len(lefts)], refs[len(lefts) + len(after) :]
        out_ref, pack_refs, refs = refs[0], refs[1 : 1 + more], refs[1 + more :]
        wide, tall, total, result, tile_sems, vector_sems, sofar_sem, out_sems = refs[:8]

        def tile_copy(t, c):
            slot = slots_ref[t, first + c + REACH]
            copy = pltpu.make_async_copy(
                tiles_ref.at[t, jnp.maximum(slot, 0)],
                wide.at[pl.ds(t * B, B), pl.ds(c * B, B)],
                tile_sems.at[t, c],
            )
            return slot >= 0, copy

        def vector_copy(c):
            return pltpu.make_async_copy(
                vectors_ref.at[pl.ds((first + c) * B, B)], tall.at[pl.ds(c * B, B)], vector_sems.at[c]
            )

        if given:
            sofar_copy = pltpu.make_async_copy(sofar_refs[0], result, sofar_sem)
        for c in range(count):
            vector_copy(c).start()
            for t in range(tiles):
                there, copy = tile_copy(t, c)
                pl.when(there)(copy.start)

                @pl.when(jnp.logical_not(there))
                def _():
                    wide[t * B : (t + 1) * B, c * B : (c + 1) * B] = jnp.zeros((B, B), jnp.bfloat16)

            if given and c == group - 1:
                sofar_copy.start()
        ins, outs = [], []
        if lefts:
            packed, in_sems, pack_sem = refs[8:]
            for d in range(shares):
                for level, ref in enumerate(left_refs):
                    ins.append(
                        pltpu.make_async_copy(
                            ref.at[pl.ds(d * rows, rows)], packed.at[d, level], in_sems.at[d, level]
                        )
                    )
            outs.append(pltpu.make_async_copy(packed, pack_refs[0], pack_sem))
            for copy in ins:
                copy.start()
        for g in range(groups):
            for c in range(g * group, (g + 1) * group):
                vector_copy(c).wait()
                for t in range(tiles):
                    there, copy = tile_copy(t, c)
                    pl.when(there)(copy.wait)
            chosen = pl.ds(g * group * B, group * B)
            if g == groups - 1:
                if given:
                    sofar_copy.wait()
                for copy in ins:
                    copy.wait()
                for copy in outs:
                    copy.start()
            for n in range(2):
                columns = pl.ds(n * half, half)
                part = jnp.dot(wide[:, chosen], tall[chosen, columns], preferred_element_type=jnp.float32)
                if g > 0:
                    part = total[:, columns] + part
                if g < groups - 1:
                    total[:, columns] = part
                else:
                    if given:
                        part = part + result[:, columns].astype(jnp.float32)
                    result[:, columns] = part.astype(jnp.bfloat16)
                    outs.append(
                        pltpu.make_async_copy(result.at[:, columns], out_ref.at[:, columns], out_sems.at[n])
                    )
                    outs[-1].start()
        for copy in outs:
            copy.wait()

    scratch = [
        pltpu.VMEM((rows, count * B), jnp.bfloat16),
        pltpu.VMEM((count * B, width), jnp.bfloat16),
        pltpu.VMEM((rows, width), jnp.float32),
        pltpu.VMEM((rows, width), jnp.bfloat16),
        pltpu.SemaphoreType.DMA((tiles, count)),
        pltpu.SemaphoreType.DMA((count,)),
        pltpu.SemaphoreType.DMA,
        pltpu.SemaphoreType.DMA((2,)),
    ]
    if lefts:
        scratch += [
            pltpu.VMEM((shares, 2, rows, rank), jnp.bfloat16),
            pltpu.SemaphoreType.DMA((shares, 2)),
            pltpu.SemaphoreType.DMA,
        ]
    return called(
        kernel,
        "near_inside",
        [slots],
        [near_tiles, vectors] + ([sofar] if given else []) + [*lefts],
        after,
        [jax.ShapeDtypeStruct((rows, width), jnp.bfloat16)]
        + [jax.ShapeDtypeStruct((shares, 2, rows, rank), jnp.bfloat16)] * more,
        scratch,
        flops=flops,
    )


def add_halos(slots, sofar, near_tiles, halos, after=()):
    rows, width = sofar.shape
    tiles = rows // B
    half = width // 2
    outside = 2 * REACH
    window = slots.shape[1]

    def kernel(slots_ref, sofar_ref, tiles_ref, *refs):
        halo_refs, refs = refs[:2], refs[2 + len(after) :]
        out_ref, wide, tall, total, result, tile_sems, halo_sems, sofar_sem, out_sems = refs
        core = lax.axis_index("cols") % 2

        def tile_copy(t, i):
            before = (i < REACH) == (core == 0)
            slot = slots_ref[t, jnp.where(before, i % REACH, window - REACH + i % REACH)]
            copy = pltpu.make_async_copy(
                tiles_ref.at[t, jnp.maximum(slot, 0)],
                wide.at[pl.ds(t * B, B), pl.ds(i * B, B)],
                tile_sems.at[t, i],
            )
            return slot >= 0, copy

        copies = [
            pltpu.make_async_copy(ref, tall.at[pl.ds(i * REACH * B, REACH * B)], halo_sems.at[i])
            for i, ref in enumerate(halo_refs)
        ]
        sofar_copy = pltpu.make_async_copy(sofar_ref, result, sofar_sem)
        for i in range(outside):
            if i % REACH == 0:
                copies[i // REACH].start()
            for t in range(tiles):
                there, copy = tile_copy(t, i)
                pl.when(there)(copy.start)

                @pl.when(jnp.logical_not(there))
                def _():
                    wide[t * B : (t + 1) * B, i * B : (i + 1) * B] = jnp.zeros((B, B), jnp.bfloat16)

        sofar_copy.start()
        out_copies = []
        for side in range(2):
            copies[side].wait()
            for i in range(side * REACH, (side + 1) * REACH):
                for t in range(tiles):
                    there, copy = tile_copy(t, i)
                    pl.when(there)(copy.wait)
            chosen = pl.ds(side * REACH * B, REACH * B)
            if side == 1:
                sofar_copy.wait()
            for n in range(2):
                columns = pl.ds(n * half, half)
                part = jnp.dot(wide[:, chosen], tall[chosen, columns], preferred_element_type=jnp.float32)
                if side == 0:
                    total[:, columns] = part
                else:
                    part = total[:, columns] + part + result[:, columns].astype(jnp.float32)
                    result[:, columns] = part.astype(jnp.bfloat16)
                    out_copies.append(
                        pltpu.make_async_copy(result.at[:, columns], out_ref.at[:, columns], out_sems.at[n])
                    )
                    out_copies[-1].start()
        for copy in out_copies:
            copy.wait()

    return called(
        kernel,
        "add_halos",
        [slots],
        [sofar, near_tiles, *halos],
        after,
        jax.ShapeDtypeStruct((rows, width), jnp.bfloat16),
        [
            pltpu.VMEM((rows, outside * B), jnp.bfloat16),
            pltpu.VMEM((outside * B, width), jnp.bfloat16),
            pltpu.VMEM((rows, width), jnp.float32),
            pltpu.VMEM((rows, width), jnp.bfloat16),
            pltpu.SemaphoreType.DMA((tiles, outside)),
            pltpu.SemaphoreType.DMA((2,)),
            pltpu.SemaphoreType.DMA,
            pltpu.SemaphoreType.DMA((2,)),
        ],
        flops=COST_C,
    )


def add_level(sofar, level, panels, coeffs):
    rows, width = sofar.shape
    half = width // 2
    offsets, _, _, rank = panels.shape
    whole = len(coeffs) == offsets
    inner = offsets * rank

    def kernel(sofar_ref, panels_ref, *refs):
        coeff_refs, refs = refs[: len(coeffs)], refs[len(coeffs) :]
        out_ref, lefts, ranks, result, left_sems, coeff_sems, sofar_sems, out_sems = refs
        mine, col = lax.axis_index("rows") % 2, lax.axis_index("cols")
        first, later = [], []
        for d in range(offsets):
            first.append(
                pltpu.make_async_copy(
                    panels_ref.at[col ^ d, level], lefts.at[:, pl.ds(d * rank, rank)], left_sems.at[d]
                )
            )
            for n in range(2):
                source = coeff_refs[d].at[pl.ds(n * rank, rank)] if whole else coeff_refs[n * offsets + d]
                (later if n else first).append(
                    pltpu.make_async_copy(source, ranks.at[n, pl.ds(d * rank, rank)], coeff_sems.at[n, d])
                )
        places = [pl.ds(n * half, half) if whole else span(mine ^ n, half) for n in range(2)]
        for n, copies in enumerate((first, later)):
            copies.append(
                pltpu.make_async_copy(sofar_ref.at[:, places[n]], result.at[n], sofar_sems.at[n])
            )
            for copy in copies:
                copy.start()
        out_copies = []
        for n, copies in enumerate((first, later)):
            for copy in copies:
                copy.wait()
            part = jnp.dot(lefts[...], ranks[n], preferred_element_type=jnp.float32)
            result[n] = (result[n].astype(jnp.float32) + part).astype(jnp.bfloat16)
            out_copies.append(
                pltpu.make_async_copy(result.at[n], out_ref.at[:, places[n]], out_sems.at[n])
            )
            out_copies[-1].start()
        for copy in out_copies:
            copy.wait()

    return called(
        kernel,
        "add_level",
        [],
        [sofar, panels, *coeffs],
        (),
        jax.ShapeDtypeStruct((rows, width), jnp.bfloat16),
        [
            pltpu.VMEM((rows, inner), jnp.bfloat16),
            pltpu.VMEM((2, inner, half), jnp.bfloat16),
            pltpu.VMEM((2, rows, half), jnp.bfloat16),
            pltpu.SemaphoreType.DMA((offsets,)),
            pltpu.SemaphoreType.DMA((2, offsets)),
            pltpu.SemaphoreType.DMA((2,)),
            pltpu.SemaphoreType.DMA((2,)),
        ],
    )


def summed(a, b, rank, swapped, passed=(), after=()):
    rows, width = a.shape
    outs = [(rank, width), (rows - rank, width)] if swapped else [(rows, width), (16, 128)]
    top = outs[0][0]

    def kernel(a_ref, b_ref, *refs):
        refs = refs[len(passed) + len(after) :]
        out_refs, (mine, theirs, total, in_sems, out_sems) = refs[: len(outs)], refs[-5:]
        ins = [
            pltpu.make_async_copy(a_ref.at[pl.ds(0, top)], mine, in_sems.at[0]),
            pltpu.make_async_copy(b_ref, theirs, in_sems.at[1]),
        ]
        for copy in ins:
            copy.start()
        for copy in ins:
            copy.wait()
        total[...] = (mine[...].astype(jnp.float32) + theirs[:top].astype(jnp.float32)).astype(jnp.bfloat16)
        results = [pltpu.make_async_copy(total, out_refs[0], out_sems.at[0])]
        other = theirs.at[pl.ds(top, rows - top)] if swapped else total.at[pl.ds(0, 16), pl.ds(0, 128)]
        results.append(pltpu.make_async_copy(other, out_refs[1], out_sems.at[1]))
        for copy in results:
            copy.start()
        for copy in results:
            copy.wait()

    return called(
        kernel,
        "summed",
        [],
        [a, b, *passed],
        after,
        [jax.ShapeDtypeStruct(shape, jnp.bfloat16) for shape in outs]
        + [jax.ShapeDtypeStruct(x.shape, x.dtype) for x in passed],
        [
            pltpu.VMEM((top, width), jnp.bfloat16),
            pltpu.VMEM((rows, width), jnp.bfloat16),
            pltpu.VMEM((top, width), jnp.bfloat16),
            pltpu.SemaphoreType.DMA((2,)),
            pltpu.SemaphoreType.DMA((2,)),
        ],
        {2 + i: len(outs) + i for i in range(len(passed))},
    )


def held(passed, after):
    def kernel(*refs):
        pass

    return called(
        kernel,
        "held",
        [],
        passed,
        after,
        [jax.ShapeDtypeStruct(x.shape, x.dtype) for x in passed],
        [],
        {i: i for i in range(len(passed))},
    )


def per_device(vectors, near_tiles, near_cols, left_one, right_one, left_two, right_two):
    n_rows, n_cols = lax.axis_size("rows"), lax.axis_size("cols")
    bits = n_rows.bit_length() - 1
    col = lax.axis_index("cols")
    depth = vectors.shape[0]
    rank = right_one.shape[1]
    inside = depth // B

    nnz = near_cols.shape[1]
    names = near_cols[:, :, None] == jnp.arange(inside + 2 * REACH, dtype=jnp.int32)
    slots = jnp.max(jnp.where(names, jnp.arange(nnz, dtype=jnp.int32)[None, :, None], -1), axis=1)

    cuts = [0, inside // 2, inside]

    def near_part(part, sofar, lefts=(), after=()):
        first, last = cuts[part : part + 2]
        return near_inside(slots, near_tiles, vectors, first, last - first, sofar, lefts, COST_B if last == inside else COST_A, after)

    send, keep, token, edge = project(right_one, right_two, vectors)
    arrived = flipped(send, 1, 0)

    (edge,) = held([edge], [flipped(token, 0, 1)])
    halo = moved(edge, lambda r, c: (r + 1 if c % 2 == 0 else r - 1, c))

    near, panels = near_part(0, None, (left_one, left_two), after=(keep,))
    both, _ = summed(keep, arrived, rank, False, after=(near,))
    for bit in range(1, bits - 2):
        both, _ = summed(both, flipped(both, 2**bit, 0), rank, False)
    arrived = flipped(both, 2 ** (bits - 2), 0)
    panels = lax.all_to_all(panels, "cols", split_axis=0, concat_axis=0, tiled=True)
    (near,) = near_part(1, near, after=(both,))
    one, two, halo = summed(both, arrived, rank, True, passed=(halo,), after=(near,))
    one = flipped(one, 2 ** (bits - 1), 0)
    near = add_halos(slots, near, near_tiles, (halo, flipped(halo, 0, 1)), after=(two,))

    offsets = range(0, n_cols, 2)
    twos = [two] + [flipped(two, 0, offset) for offset in offsets[1:]]
    one, *rest = held([one, *twos[1:]], [near])
    twos = [two] + rest
    ones = [
        one if (other, offset) == (0, 0) else flipped(one, other, offset)
        for other in range(2)
        for offset in offsets
    ]
    coeffs_two = [x for there in twos for x in (there, flipped(there, 0, 1))]
    near = add_level(near, 1, panels, coeffs_two)
    ones = [one, *held(ones[1:], [near])]
    coeffs_one = [x for there in ones for x in (there, flipped(there, 0, 1))]
    return add_level(near, 0, panels, coeffs_one)


def solution(mesh):
    placed = (
        P("rows", None),
        P(("rows", "cols"), None, None, None),
        P(("rows", "cols"), None),
        P("rows", "cols"),
        P("rows", "cols"),
        P("rows", "cols"),
        P("rows", "cols"),
    )
    return jax.shard_map(
        per_device, mesh=mesh, in_specs=placed, out_specs=P(("rows", "cols"), None), check_vma=False
    )
```

```python
import jax
import jax.numpy as jnp
from jax import lax
from jax.experimental import pallas as pl
from jax.experimental.pallas import tpu as pltpu
from jax.sharding import PartitionSpec as P

B = 256
REACH = 2
AXES = ("rows", "cols")
VMEM = 64 * 1024 * 1024
COST_A = 1
COST_B = 1
COST_C = 7000000000
HBM = pl.BlockSpec(memory_space=pltpu.HBM)
SMEM = pl.BlockSpec(memory_space=pltpu.SMEM)


def moved(value, target):
    n_rows, n_cols = lax.axis_size("rows"), lax.axis_size("cols")
    pairs = []
    for row in range(n_rows):
        for col in range(n_cols):
            other = target(row, col)
            if other is not None and 0 <= other[0] < n_rows:
                pairs.append((row * n_cols + col, other[0] * n_cols + other[1]))
    return lax.ppermute(value, AXES, pairs)


def flipped(value, row_bits, col_bits):
    return moved(value, lambda row, col: (row ^ row_bits, col ^ col_bits))


def span(index, size):
    return pl.ds(pl.multiple_of(index * size, size), size)


def called(kernel, name, smem, hbm, after, out_shape, scratch, aliases={}, flops=1):
    return pl.pallas_call(
        kernel,
        out_shape=out_shape,
        in_specs=[SMEM] * len(smem) + [HBM] * (len(hbm) + len(after)),
        out_specs=jax.tree.map(lambda _: HBM, out_shape),
        scratch_shapes=scratch,
        input_output_aliases=aliases,
        compiler_params=pltpu.CompilerParams(vmem_limit_bytes=VMEM),
        cost_estimate=pl.CostEstimate(flops=flops, bytes_accessed=1, transcendentals=0),
        name=name,
    )(*smem, *hbm, *after)


def project(right_one, right_two, vectors):
    depth, rank = right_one.shape
    width = vectors.shape[1]
    half = width // 2
    step = REACH * B
    parts = depth // step

    def kernel(one_ref, two_ref, vectors_ref, send_ref, keep_ref, edge_ref, *scratch):
        rights, block, total, result, right_sems, block_sems, out_sems, edge_sem = scratch
        mine, last_first = lax.axis_index("rows") % 2, lax.axis_index("cols") % 2 == 0
        copies, places = [], []
        for i in range(parts):
            place = span(jnp.where(last_first, parts - 1 - i, i), step)
            places.append(place)
            copies.append(
                [
                    pltpu.make_async_copy(
                        ref.at[place], rights.at[place, pl.ds(level * rank, rank)], right_sems.at[level, i]
                    )
                    for level, ref in enumerate((one_ref, two_ref))
                ]
                + [pltpu.make_async_copy(vectors_ref.at[place], block.at[place], block_sems.at[i])]
            )
            for copy in copies[-1]:
                copy.start()
        edge_copy = pltpu.make_async_copy(block.at[places[0]], edge_ref, edge_sem)
        for i in range(parts):
            for copy in copies[i]:
                copy.wait()
            if i == 0:
                edge_copy.start()
            part = lax.dot_general(
                rights[places[i]], block[places[i]], (((0,), (0,)), ((), ())), preferred_element_type=jnp.float32
            )
            if i == 0:
                total[...] = part
            elif i < parts - 1:
                total[...] += part
            else:
                result[...] = (total[...] + part).astype(jnp.bfloat16)
        outs = []
        for k, (ref, chosen) in enumerate(((send_ref, mine ^ 1), (keep_ref, mine))):
            outs.append(
                pltpu.make_async_copy(
                    result.at[pl.ds(0, rank), span(chosen, half)], ref.at[pl.ds(0, rank)], out_sems.at[k, 0]
                )
            )
            for n in range(2):
                outs.append(
                    pltpu.make_async_copy(
                        result.at[pl.ds(rank, rank), pl.ds(n * half, half)],
                        ref.at[pl.ds((1 + n) * rank, rank)],
                        out_sems.at[k, 1 + n],
                    )
                )
        for copy in outs:
            copy.start()
        for copy in outs:
            copy.wait()
        edge_copy.wait()

    return called(
        kernel,
        "project",
        [],
        [right_one, right_two, vectors],
        (),
        [
            jax.ShapeDtypeStruct((3 * rank, half), jnp.bfloat16),
            jax.ShapeDtypeStruct((3 * rank, half), jnp.bfloat16),
            jax.ShapeDtypeStruct((step, width), jnp.bfloat16),
        ],
        [
            pltpu.VMEM((depth, 2 * rank), jnp.bfloat16),
            pltpu.VMEM((depth, width), jnp.bfloat16),
            pltpu.VMEM((2 * rank, width), jnp.float32),
            pltpu.VMEM((2 * rank, width), jnp.bfloat16),
            pltpu.SemaphoreType.DMA((2, parts)),
            pltpu.SemaphoreType.DMA((parts,)),
            pltpu.SemaphoreType.DMA((2, 3)),
            pltpu.SemaphoreType.DMA,
        ],
    )


def near_field(near_cols, near_tiles, vectors, first, count, sofar=None, halos=(), after=(), flops=1):
    tiles, nnz = near_cols.shape
    rows, width = tiles * B, vectors.shape[1]
    window = vectors.shape[0] // B + 2 * REACH
    half = width // 2
    given = 0 if sofar is None else 1
    inside = count
    if halos:
        count += 2 * REACH
    sizes = []
    while sum(sizes) < inside:
        sizes.append(min((1, 3, 4)[min(len(sizes), 2)], inside - sum(sizes)))
    if inside and sizes[-1] == 1:
        sizes = sizes[:-2] + [sizes[-2] + 1] if len(sizes) > 1 else sizes
    if halos:
        sizes += [REACH, REACH]
    groups = len(sizes)
    begins = [sum(sizes[:g]) for g in range(groups)]

    def kernel(cols_ref, tiles_ref, vectors_ref, *refs):
        sofar_refs, refs = refs[:given], refs[given:]
        halo_refs, refs = refs[: len(halos)], refs[len(halos) + len(after) :]
        out_ref, slots, wide, tall, total, result, tile_sems, tall_sems, sofar_sem, out_sems = refs
        col = lax.axis_index("cols")

        for t in range(tiles):
            for c in range(window):
                slots[t, c] = -1
            for k in range(nnz):
                slots[t, cols_ref[t, k]] = k

        def tile_copy(t, c):
            if c < inside:
                place = first + c + REACH
            else:
                i = c - inside
                before = (i < REACH) == (col % 2 == 1)
                place = jnp.where(before, i % REACH, window - REACH + i % REACH)
            slot = slots[t, place]
            copy = pltpu.make_async_copy(
                tiles_ref.at[t, jnp.maximum(slot, 0)],
                wide.at[pl.ds(t * B, B), pl.ds(c * B, B)],
                tile_sems.at[t, c],
            )
            return slot >= 0, copy

        def tall_copy(g):
            place = pl.ds(begins[g] * B, sizes[g] * B)
            if begins[g] < inside:
                source = vectors_ref.at[pl.ds((first + begins[g]) * B, sizes[g] * B)]
            else:
                source = halo_refs[g - groups]
            return pltpu.make_async_copy(source, tall.at[place], tall_sems.at[g])

        if given:
            sofar_copy = pltpu.make_async_copy(sofar_refs[0], result, sofar_sem)
        for g in range(groups):
            tall_copy(g).start()
            for c in range(begins[g], begins[g] + sizes[g]):
                for t in range(tiles):
                    there, copy = tile_copy(t, c)
                    pl.when(there)(copy.start)

                    @pl.when(jnp.logical_not(there))
                    def _():
                        wide[t * B : (t + 1) * B, c * B : (c + 1) * B] = jnp.zeros((B, B), jnp.bfloat16)

        if given:
            sofar_copy.start()
        outs = []
        for g in range(groups):
            tall_copy(g).wait()
            for c in range(begins[g], begins[g] + sizes[g]):
                for t in range(tiles):
                    there, copy = tile_copy(t, c)
                    pl.when(there)(copy.wait)
            chosen = pl.ds(begins[g] * B, sizes[g] * B)
            if g == groups - 1:
                if given:
                    sofar_copy.wait()
            for n in range(2):
                columns = pl.ds(n * half, half)
                part = jnp.dot(wide[:, chosen], tall[chosen, columns], preferred_element_type=jnp.float32)
                if g > 0:
                    part = total[:, columns] + part
                if g < groups - 1:
                    total[:, columns] = part
                else:
                    if given:
                        part = part + result[:, columns].astype(jnp.float32)
                    result[:, columns] = part.astype(jnp.bfloat16)
                    outs.append(
                        pltpu.make_async_copy(result.at[:, columns], out_ref.at[:, columns], out_sems.at[n])
                    )
                    outs[-1].start()
        for copy in outs:
            copy.wait()

    scratch = [
        pltpu.SMEM((tiles, window), jnp.int32),
        pltpu.VMEM((rows, count * B), jnp.bfloat16),
        pltpu.VMEM((count * B, width), jnp.bfloat16),
        pltpu.VMEM((rows, width), jnp.float32),
        pltpu.VMEM((rows, width), jnp.bfloat16),
        pltpu.SemaphoreType.DMA((tiles, count)),
        pltpu.SemaphoreType.DMA((groups,)),
        pltpu.SemaphoreType.DMA,
        pltpu.SemaphoreType.DMA((2,)),
    ]
    return called(
        kernel,
        "near_field",
        [near_cols],
        [near_tiles, vectors] + ([sofar] if given else []) + [*halos],
        after,
        jax.ShapeDtypeStruct((rows, width), jnp.bfloat16),
        scratch,
        flops=flops,
    )


def packed(lefts, shares, after):
    depth, rank = lefts[0].shape
    rows = depth // shares

    def kernel(one_ref, two_ref, *refs):
        refs = refs[len(after) :]
        out_refs, (block, in_sems, out_sems) = refs[: shares - 1], refs[shares - 1 :]
        col = lax.axis_index("cols")
        ins = [
            [
                pltpu.make_async_copy(
                    ref.at[span(col ^ (d + 1), rows)], block.at[d, level], in_sems.at[d, level]
                )
                for level, ref in enumerate((one_ref, two_ref))
            ]
            for d in range(shares - 1)
        ]
        for copies in ins:
            for copy in copies:
                copy.start()
        outs = []
        for d in range(shares - 1):
            for copy in ins[d]:
                copy.wait()
            outs.append(pltpu.make_async_copy(block.at[d], out_refs[d], out_sems.at[d]))
            outs[-1].start()
        for copy in outs:
            copy.wait()

    return called(
        kernel,
        "packed",
        [],
        [*lefts],
        after,
        [jax.ShapeDtypeStruct((2, rows, rank), jnp.bfloat16)] * (shares - 1),
        [
            pltpu.VMEM((shares - 1, 2, rows, rank), jnp.bfloat16),
            pltpu.SemaphoreType.DMA((shares - 1, 2)),
            pltpu.SemaphoreType.DMA((shares - 1,)),
        ],
    )


def add_levels(sofar, lefts, pieces, coeffs_one, coeffs_two):
    rows, width = sofar.shape
    half = width // 2
    rank = lefts[0].shape[1]
    offsets = len(pieces) + 1
    inner = 2 * offsets * rank

    def kernel(sofar_ref, *refs):
        left_refs, piece_refs, refs = refs[:2], refs[2 : 1 + offsets], refs[1 + offsets :]
        one_refs, refs = refs[: 2 * offsets], refs[2 * offsets :]
        two_refs, refs = refs[:offsets], refs[offsets:]
        out_ref, wide, ranks, result, left_sems, rank_sems, sofar_sems, out_sems = refs
        mine, col = lax.axis_index("rows") % 2, lax.axis_index("cols")
        places = [span(mine ^ n, half) for n in range(2)]
        copies = [[], []]
        for d in range(offsets):
            for level in range(2):
                place = pl.ds((level * offsets + d) * rank, rank)
                source = piece_refs[d - 1].at[level] if d else left_refs[level].at[span(col, rows)]
                copies[0].append(pltpu.make_async_copy(source, wide.at[:, place], left_sems.at[level, d]))
                for n in range(2):
                    source = two_refs[d].at[span(mine ^ n, rank)] if level else one_refs[n * offsets + d]
                    copies[n].append(
                        pltpu.make_async_copy(source, ranks.at[n, place], rank_sems.at[n, level, d])
                    )
        for n in range(2):
            copies[n].append(
                pltpu.make_async_copy(sofar_ref.at[:, places[n]], result.at[n], sofar_sems.at[n])
            )
            for copy in copies[n]:
                copy.start()
        outs = []
        for n in range(2):
            for copy in copies[n]:
                copy.wait()
            part = jnp.dot(wide[...], ranks[n], preferred_element_type=jnp.float32)
            result[n] = (result[n].astype(jnp.float32) + part).astype(jnp.bfloat16)
            outs.append(pltpu.make_async_copy(result.at[n], out_ref.at[:, places[n]], out_sems.at[n]))
            outs[-1].start()
        for copy in outs:
            copy.wait()

    return called(
        kernel,
        "add_levels",
        [],
        [sofar, *lefts, *pieces, *coeffs_one, *coeffs_two],
        (),
        jax.ShapeDtypeStruct((rows, width), jnp.bfloat16),
        [
            pltpu.VMEM((rows, inner), jnp.bfloat16),
            pltpu.VMEM((2, inner, half), jnp.bfloat16),
            pltpu.VMEM((2, rows, half), jnp.bfloat16),
            pltpu.SemaphoreType.DMA((2, offsets)),
            pltpu.SemaphoreType.DMA((2, 2, offsets)),
            pltpu.SemaphoreType.DMA((2,)),
            pltpu.SemaphoreType.DMA((2,)),
        ],
    )


def parted(a, b, top):
    rows, width = b.shape

    def kernel(a_ref, b_ref, sum_ref, rest_ref, mine, theirs, total, sems):
        ins = [
            pltpu.make_async_copy(a_ref.at[pl.ds(0, top)], mine, sems.at[0]),
            pltpu.make_async_copy(b_ref.at[pl.ds(0, top)], theirs.at[pl.ds(0, top)], sems.at[1]),
            pltpu.make_async_copy(
                b_ref.at[pl.ds(top, rows - top)], theirs.at[pl.ds(top, rows - top)], sems.at[2]
            ),
        ]
        for copy in ins:
            copy.start()
        ins[0].wait()
        ins[1].wait()
        total[...] = (mine[...].astype(jnp.float32) + theirs[:top].astype(jnp.float32)).astype(jnp.bfloat16)
        outs = [
            pltpu.make_async_copy(total, sum_ref, sems.at[3]),
            pltpu.make_async_copy(theirs.at[pl.ds(top, rows - top)], rest_ref, sems.at[4]),
        ]
        outs[0].start()
        ins[2].wait()
        outs[1].start()
        for copy in outs:
            copy.wait()

    return called(
        kernel,
        "parted",
        [],
        [a, b],
        (),
        [
            jax.ShapeDtypeStruct((top, width), jnp.bfloat16),
            jax.ShapeDtypeStruct((rows - top, width), jnp.bfloat16),
        ],
        [
            pltpu.VMEM((top, width), jnp.bfloat16),
            pltpu.VMEM((rows, width), jnp.bfloat16),
            pltpu.VMEM((top, width), jnp.bfloat16),
            pltpu.SemaphoreType.DMA((5,)),
        ],
    )


def held(passed, after):
    def kernel(*refs):
        pass

    return called(
        kernel,
        "held",
        [],
        passed,
        after,
        [jax.ShapeDtypeStruct(x.shape, x.dtype) for x in passed],
        [],
        {i: i for i in range(len(passed))},
    )


def per_device(vectors, near_tiles, near_cols, left_one, right_one, left_two, right_two):
    n_rows, n_cols = lax.axis_size("rows"), lax.axis_size("cols")
    bits = n_rows.bit_length() - 1
    col = lax.axis_index("cols")
    depth = vectors.shape[0]
    rank = right_one.shape[1]
    inside = depth // B

    near_args = (near_cols, near_tiles, vectors)
    cuts = [0, inside // 8, 9 * inside // 16, inside]

    def near_part(part, sofar, after, flops):
        first, last = cuts[part : part + 2]
        return near_field(*near_args, first, last - first, sofar, after=after, flops=flops)

    def summed(a, b):
        return (a.astype(jnp.float32) + b.astype(jnp.float32)).astype(jnp.bfloat16)

    send, keep, edge = project(right_one, right_two, vectors)
    arrived = flipped(send, 1, 0)

    pieces = packed((left_one, left_two), n_cols, (keep,))
    pieces = [flipped(piece, 0, offset) for offset, piece in enumerate(pieces, 1)]

    near = near_part(0, None, (keep,), COST_A)
    (keep,) = held([keep], [near])
    both = summed(keep, arrived)
    for bit in range(1, bits - 2):
        both = summed(both, flipped(both, 2**bit, 0))
    arrived = flipped(both, 2 ** (bits - 2), 0)

    (edge,) = held([edge], [both])
    halo = moved(edge, lambda r, c: (r + 1 if c % 2 == 0 else r - 1, c ^ 1))
    near = near_part(1, near, (both,), COST_B)
    both, *pieces[:-1] = held([both, *pieces[:-1]], [near])
    one, two = parted(both, arrived, rank)
    one = flipped(one, 2 ** (bits - 1), 0)
    near = near_part(2, near, (two,), COST_C)

    offsets = range(0, n_cols, 2)
    twos = [two] + [flipped(two, 0, offset) for offset in offsets[1:]]
    one, halo, pieces[-1], *rest = held([one, halo, pieces[-1], *twos[1:]], [near])
    twos = [two] + rest
    ones = [
        one if (other, offset) == (0, 0) else flipped(one, other, offset)
        for other in range(2)
        for offset in offsets
    ]
    near = near_field(*near_args, 0, 0, near, (halo, flipped(halo, 0, 1)))
    ones = [one, *held(ones[1:], [near])]
    coeffs_two = [x for there in twos for x in (there, flipped(there, 0, 1))]
    coeffs_one = [x for there in ones for x in (there, flipped(there, 0, 1))]
    return add_levels(near, (left_one, left_two), pieces, coeffs_one, coeffs_two)


def solution(mesh):
    placed = (
        P("rows", None),
        P(("rows", "cols"), None, None, None),
        P(("rows", "cols"), None),
        P("rows", "cols"),
        P("rows", "cols"),
        P("rows", "cols"),
        P("rows", "cols"),
    )
    return jax.shard_map(
        per_device, mesh=mesh, in_specs=placed, out_specs=P(("rows", "cols"), None), check_vma=False
    )
```

```python
import jax
import jax.numpy as jnp
from jax import lax
from jax.experimental import pallas as pl
from jax.experimental.pallas import tpu as pltpu
from jax.sharding import PartitionSpec as P

B = 256
REACH = 2
AXES = ("rows", "cols")
VMEM = 64 * 1024 * 1024
COST_A = 1
COST_B = 1
COST_C = int(7000000000.0)
COST_D = int(10000000000.0)
HBM = pl.BlockSpec(memory_space=pltpu.HBM)
SMEM = pl.BlockSpec(memory_space=pltpu.SMEM)


def moved(value, target):
    n_rows, n_cols = lax.axis_size("rows"), lax.axis_size("cols")
    pairs = []
    for row in range(n_rows):
        for col in range(n_cols):
            other = target(row, col)
            if other is not None and 0 <= other[0] < n_rows:
                pairs.append((row * n_cols + col, other[0] * n_cols + other[1]))
    return lax.ppermute(value, AXES, pairs)


def flipped(value, row_bits, col_bits):
    return moved(value, lambda row, col: (row ^ row_bits, col ^ col_bits))


def span(index, size):
    return pl.ds(pl.multiple_of(index * size, size), size)


def called(kernel, name, smem, hbm, after, out_shape, scratch, aliases={}, flops=1):
    return pl.pallas_call(
        kernel,
        out_shape=out_shape,
        in_specs=[SMEM] * len(smem) + [HBM] * (len(hbm) + len(after)),
        out_specs=jax.tree.map(lambda _: HBM, out_shape),
        scratch_shapes=scratch,
        input_output_aliases=aliases,
        compiler_params=pltpu.CompilerParams(vmem_limit_bytes=VMEM),
        cost_estimate=pl.CostEstimate(flops=flops, bytes_accessed=1, transcendentals=0),
        name=name,
    )(*smem, *hbm, *after)


def project(right_one, right_two, vectors):
    depth, rank = right_one.shape
    width = vectors.shape[1]
    half = width // 2
    step = REACH * B
    parts = depth // step

    def kernel(one_ref, two_ref, vectors_ref, send_ref, keep_ref, *scratch):
        rights, block, total, result, right_sems, block_sems, out_sems = scratch
        mine = lax.axis_index("rows") % 2
        copies, places = [], []
        for i in range(parts):
            place = pl.ds(i * step, step)
            places.append(place)
            copies.append(
                [
                    pltpu.make_async_copy(
                        ref.at[place], rights.at[place, pl.ds(level * rank, rank)], right_sems.at[level, i]
                    )
                    for level, ref in enumerate((one_ref, two_ref))
                ]
                + [pltpu.make_async_copy(vectors_ref.at[place], block.at[place], block_sems.at[i])]
            )
            for copy in copies[-1]:
                copy.start()
        for i in range(parts):
            for copy in copies[i]:
                copy.wait()
            part = lax.dot_general(
                rights[places[i]], block[places[i]], (((0,), (0,)), ((), ())), preferred_element_type=jnp.float32
            )
            if i == 0:
                total[...] = part
            elif i < parts - 1:
                total[...] += part
            else:
                result[...] = (total[...] + part).astype(jnp.bfloat16)
        outs = []
        for k, (ref, chosen) in enumerate(((send_ref, mine ^ 1), (keep_ref, mine))):
            outs.append(
                pltpu.make_async_copy(
                    result.at[pl.ds(0, rank), span(chosen, half)], ref.at[pl.ds(0, rank)], out_sems.at[k, 0]
                )
            )
            for n in range(2):
                outs.append(
                    pltpu.make_async_copy(
                        result.at[pl.ds(rank, rank), pl.ds(n * half, half)],
                        ref.at[pl.ds((1 + n) * rank, rank)],
                        out_sems.at[k, 1 + n],
                    )
                )
        for copy in outs:
            copy.start()
        for copy in outs:
            copy.wait()

    return called(
        kernel,
        "project",
        [],
        [right_one, right_two, vectors],
        (),
        [
            jax.ShapeDtypeStruct((3 * rank, half), jnp.bfloat16),
            jax.ShapeDtypeStruct((3 * rank, half), jnp.bfloat16),
        ],
        [
            pltpu.VMEM((depth, 2 * rank), jnp.bfloat16),
            pltpu.VMEM((depth, width), jnp.bfloat16),
            pltpu.VMEM((2 * rank, width), jnp.float32),
            pltpu.VMEM((2 * rank, width), jnp.bfloat16),
            pltpu.SemaphoreType.DMA((2, parts)),
            pltpu.SemaphoreType.DMA((parts,)),
            pltpu.SemaphoreType.DMA((2, 3)),
        ],
    )


def near_field(near_cols, near_tiles, vectors, first, count, sofar=None, halos=(), low_rank=None, after=(), flops=1):
    tiles, nnz = near_cols.shape
    rows, width = tiles * B, vectors.shape[1]
    half = width // 2
    window = vectors.shape[0] // B + 2 * REACH
    inside = count
    given = 0 if sofar is None else 1
    sizes = []
    while sum(sizes) < inside:
        sizes.append(min((1, 3, 4)[min(len(sizes), 2)], inside - sum(sizes)))
    if halos:
        sizes += [REACH, REACH]
    count = sum(sizes)
    near_groups = len(sizes)
    begins = [sum(sizes[:g]) * B for g in range(near_groups)] + [count * B]
    level, own, pieces, coeffs = low_rank or (0, None, (), ())
    rank = own.shape[1] if low_rank else 0
    offsets = len(pieces) + 1 if low_rank else 0
    whole = len(coeffs) == offsets
    depths = [size * B for size in sizes] + ([offsets * rank] if low_rank else [])
    groups, depth = len(depths), sum(depths)
    bound = [*halos, *([own, *pieces, *coeffs] if low_rank else [])]

    def kernel(cols_ref, tiles_ref, vectors_ref, *refs):
        sofar_refs, refs = refs[:given], refs[given:]
        halo_refs, refs = refs[: len(halos)], refs[len(halos) :]
        left_refs, refs = refs[:offsets], refs[offsets:]
        coeff_refs, refs = refs[: len(coeffs)], refs[len(coeffs) + len(after) :]
        out_ref, slots, wide, tall, total, result, *refs = refs
        tile_sems, tall_sems, rank_sems, sofar_sem, out_sems = refs
        mine, col = lax.axis_index("rows") % 2, lax.axis_index("cols")

        if count:
            for t in range(tiles):
                for c in range(window):
                    slots[t, c] = -1
                for k in range(nnz):
                    slots[t, cols_ref[t, k]] = k

        def tile_copy(t, c):
            if c < inside:
                place = first + c + REACH
            else:
                i = c - inside
                before = (i < REACH) == (col % 2 == 1)
                place = jnp.where(before, i % REACH, window - REACH + i % REACH)
            slot = slots[t, place]
            copy = pltpu.make_async_copy(
                tiles_ref.at[t, jnp.maximum(slot, 0)],
                wide.at[pl.ds(t * B, B), pl.ds(c * B, B)],
                tile_sems.at[t, c],
            )
            return slot >= 0, copy

        def group_tiles(g):
            return [(t, c) for c in range(begins[g] // B, begins[g] // B + sizes[g]) for t in range(tiles)]

        def tall_copy(g):
            if begins[g] < inside * B:
                source = vectors_ref.at[pl.ds(first * B + begins[g], depths[g])]
            else:
                source = halo_refs[g - near_groups]
            return pltpu.make_async_copy(source, tall.at[pl.ds(begins[g], depths[g])], tall_sems.at[g])

        rank_copies = []
        for d in range(offsets):
            source = left_refs[d].at[level] if d else left_refs[0].at[span(col, rows)]
            place = pl.ds(count * B + d * rank, rank)
            rank_copies.append(pltpu.make_async_copy(source, wide.at[:, place], rank_sems.at[d, 2]))
            for n in range(2):
                if whole:
                    source, columns = coeff_refs[d].at[pl.ds(n * rank, rank)], pl.ds(n * half, half)
                else:
                    source, columns = coeff_refs[n * offsets + d], span(mine ^ n, half)
                rank_copies.append(pltpu.make_async_copy(source, tall.at[place, columns], rank_sems.at[d, n]))
        if given:
            sofar_copy = pltpu.make_async_copy(sofar_refs[0], result, sofar_sem)

        for g in range(near_groups):
            tall_copy(g).start()
            for t, c in group_tiles(g):
                there, copy = tile_copy(t, c)
                pl.when(there)(copy.start)

                @pl.when(jnp.logical_not(there))
                def _():
                    wide[t * B : (t + 1) * B, c * B : (c + 1) * B] = jnp.zeros((B, B), jnp.bfloat16)

        for copy in rank_copies:
            copy.start()
        if given:
            sofar_copy.start()
        outs = []
        for g in range(groups):
            last = g == groups - 1
            if g < near_groups:
                tall_copy(g).wait()
                for t, c in group_tiles(g):
                    there, copy = tile_copy(t, c)
                    pl.when(there)(copy.wait)
            else:
                for copy in rank_copies:
                    copy.wait()
            if last:
                if given:
                    sofar_copy.wait()
            chosen = pl.ds(begins[g], depths[g])
            cuts = 4 if last else 2
            for n in range(cuts):
                columns = pl.ds(n * (width // cuts), width // cuts)
                part = jnp.dot(wide[:, chosen], tall[chosen, columns], preferred_element_type=jnp.float32)
                if g > 0:
                    part = total[:, columns] + part
                if not last:
                    total[:, columns] = part
                else:
                    if given:
                        part = part + result[:, columns].astype(jnp.float32)
                    result[:, columns] = part.astype(jnp.bfloat16)
                    outs.append(
                        pltpu.make_async_copy(result.at[:, columns], out_ref.at[:, columns], out_sems.at[n])
                    )
                    outs[-1].start()
        for copy in outs:
            copy.wait()

    scratch = [
        pltpu.SMEM((tiles, window), jnp.int32),
        pltpu.VMEM((rows, depth), jnp.bfloat16),
        pltpu.VMEM((depth, width), jnp.bfloat16),
        pltpu.VMEM((rows, width), jnp.float32),
        pltpu.VMEM((rows, width), jnp.bfloat16),
        pltpu.SemaphoreType.DMA((tiles, max(count, 1))),
        pltpu.SemaphoreType.DMA((groups,)),
        pltpu.SemaphoreType.DMA((max(offsets, 1), 3)),
        pltpu.SemaphoreType.DMA,
        pltpu.SemaphoreType.DMA((4,)),
    ]
    return called(
        kernel,
        "near_field",
        [near_cols],
        [near_tiles, vectors] + ([sofar] if given else []) + bound,
        after,
        jax.ShapeDtypeStruct((rows, width), jnp.bfloat16),
        scratch,
        flops=flops,
    )


def packed(vectors, lefts, shares, after):
    depth, rank = lefts[0].shape
    rows = depth // shares

    edge, width = REACH * B, vectors.shape[1]

    def kernel(vectors_ref, one_ref, two_ref, *refs):
        refs = refs[len(after) :]
        edge_ref, out_refs, (rows_held, block, edge_sems, in_sems, out_sems) = refs[0], refs[1:shares], refs[shares:]
        col = lax.axis_index("cols")
        place = span(jnp.where(col % 2 == 0, depth // edge - 1, 0), edge)
        edge_in = pltpu.make_async_copy(vectors_ref.at[place], rows_held, edge_sems.at[0])
        edge_out = pltpu.make_async_copy(rows_held, edge_ref, edge_sems.at[1])
        ins = [
            [
                pltpu.make_async_copy(
                    ref.at[span(col ^ (d + 1), rows)], block.at[d, level], in_sems.at[d, level]
                )
                for level, ref in enumerate((one_ref, two_ref))
            ]
            for d in range(shares - 1)
        ]
        for copies in ins:
            for copy in copies:
                copy.start()
        edge_in.start()
        outs = []
        for d in range(shares - 1):
            for copy in ins[d]:
                copy.wait()
            outs.append(pltpu.make_async_copy(block.at[d], out_refs[d], out_sems.at[d]))
            outs[-1].start()
        edge_in.wait()
        edge_out.start()
        outs.append(edge_out)
        for copy in outs:
            copy.wait()

    return called(
        kernel,
        "packed",
        [],
        [vectors, *lefts],
        after,
        [jax.ShapeDtypeStruct((edge, width), jnp.bfloat16)]
        + [jax.ShapeDtypeStruct((2, rows, rank), jnp.bfloat16)] * (shares - 1),
        [
            pltpu.VMEM((edge, width), jnp.bfloat16),
            pltpu.VMEM((shares - 1, 2, rows, rank), jnp.bfloat16),
            pltpu.SemaphoreType.DMA((2,)),
            pltpu.SemaphoreType.DMA((shares - 1, 2)),
            pltpu.SemaphoreType.DMA((shares - 1,)),
        ],
    )


def add_level(sofar, level, own, pieces, coeffs, after=()):
    rows, width = sofar.shape
    half = width // 2
    rank = own.shape[1]
    offsets = len(pieces) + 1
    inner = offsets * rank

    def kernel(sofar_ref, own_ref, *refs):
        piece_refs, refs = refs[: offsets - 1], refs[offsets - 1 :]
        coeff_refs, refs = refs[:offsets], refs[offsets + len(after) :]
        out_ref, lefts, ranks, result, left_sems, rank_sems, sofar_sems, out_sems = refs
        col = lax.axis_index("cols")
        places = [pl.ds(n * half, half) for n in range(2)]
        copies = [[], []]
        for d in range(offsets):
            place = pl.ds(d * rank, rank)
            source = piece_refs[d - 1].at[level] if d else own_ref.at[span(col, rows)]
            copies[0].append(pltpu.make_async_copy(source, lefts.at[:, place], left_sems.at[d]))
            for n in range(2):
                source = coeff_refs[d].at[pl.ds(n * rank, rank)]
                copies[n].append(pltpu.make_async_copy(source, ranks.at[n, place], rank_sems.at[n, d]))
        for n in range(2):
            copies[n].append(
                pltpu.make_async_copy(sofar_ref.at[:, places[n]], result.at[n], sofar_sems.at[n])
            )
            for copy in copies[n]:
                copy.start()
        outs = []
        for n in range(2):
            for copy in copies[n]:
                copy.wait()
            part = jnp.dot(lefts[...], ranks[n], preferred_element_type=jnp.float32)
            result[n] = (result[n].astype(jnp.float32) + part).astype(jnp.bfloat16)
            outs.append(pltpu.make_async_copy(result.at[n], out_ref.at[:, places[n]], out_sems.at[n]))
            outs[-1].start()
        for copy in outs:
            copy.wait()

    return called(
        kernel,
        "add_level",
        [],
        [sofar, own, *pieces, *coeffs],
        after,
        jax.ShapeDtypeStruct((rows, width), jnp.bfloat16),
        [
            pltpu.VMEM((rows, inner), jnp.bfloat16),
            pltpu.VMEM((2, inner, half), jnp.bfloat16),
            pltpu.VMEM((2, rows, half), jnp.bfloat16),
            pltpu.SemaphoreType.DMA((offsets,)),
            pltpu.SemaphoreType.DMA((2, offsets)),
            pltpu.SemaphoreType.DMA((2,)),
            pltpu.SemaphoreType.DMA((2,)),
        ],
        flops=COST_D,
    )


def parted(a, b, top):
    rows, width = b.shape

    def kernel(a_ref, b_ref, sum_ref, rest_ref, mine, theirs, total, sems):
        ins = [
            pltpu.make_async_copy(a_ref.at[pl.ds(0, top)], mine, sems.at[0]),
            pltpu.make_async_copy(b_ref.at[pl.ds(0, top)], theirs.at[pl.ds(0, top)], sems.at[1]),
            pltpu.make_async_copy(
                b_ref.at[pl.ds(top, rows - top)], theirs.at[pl.ds(top, rows - top)], sems.at[2]
            ),
        ]
        for copy in ins:
            copy.start()
        ins[0].wait()
        ins[1].wait()
        total[...] = (mine[...].astype(jnp.float32) + theirs[:top].astype(jnp.float32)).astype(jnp.bfloat16)
        outs = [
            pltpu.make_async_copy(total, sum_ref, sems.at[3]),
            pltpu.make_async_copy(theirs.at[pl.ds(top, rows - top)], rest_ref, sems.at[4]),
        ]
        outs[0].start()
        ins[2].wait()
        outs[1].start()
        for copy in outs:
            copy.wait()

    return called(
        kernel,
        "parted",
        [],
        [a, b],
        (),
        [
            jax.ShapeDtypeStruct((top, width), jnp.bfloat16),
            jax.ShapeDtypeStruct((rows - top, width), jnp.bfloat16),
        ],
        [
            pltpu.VMEM((top, width), jnp.bfloat16),
            pltpu.VMEM((rows, width), jnp.bfloat16),
            pltpu.VMEM((top, width), jnp.bfloat16),
            pltpu.SemaphoreType.DMA((5,)),
        ],
    )


def held(passed, after):
    def kernel(*refs):
        pass

    return called(
        kernel,
        "held",
        [],
        passed,
        after,
        [jax.ShapeDtypeStruct(x.shape, x.dtype) for x in passed],
        [],
        {i: i for i in range(len(passed))},
    )


def per_device(vectors, near_tiles, near_cols, left_one, right_one, left_two, right_two):
    n_rows, n_cols = lax.axis_size("rows"), lax.axis_size("cols")
    bits = n_rows.bit_length() - 1
    col = lax.axis_index("cols")
    depth = vectors.shape[0]
    rank = right_one.shape[1]
    inside = depth // B

    near_args = (near_cols, near_tiles, vectors)
    cuts = [0, inside // 4, 11 * inside // 16, inside]

    def near_part(part, sofar, after, flops):
        first, last = cuts[part : part + 2]
        return near_field(*near_args, first, last - first, sofar, after=after, flops=flops)

    def summed(a, b):
        return (a.astype(jnp.float32) + b.astype(jnp.float32)).astype(jnp.bfloat16)

    send, keep = project(right_one, right_two, vectors)
    arrived = flipped(send, 1, 0)

    edge, *pieces = packed(vectors, (left_one, left_two), n_cols, (keep,))
    pieces = [flipped(piece, 0, offset) for offset, piece in enumerate(pieces, 1)]

    near = near_part(0, None, (keep,), COST_A)
    (keep,) = held([keep], [near])
    both = summed(keep, arrived)
    for bit in range(1, bits - 2):
        both = summed(both, flipped(both, 2**bit, 0))
    arrived = flipped(both, 2 ** (bits - 2), 0)

    (edge,) = held([edge], [both])
    halo = moved(edge, lambda r, c: (r + 1 if c % 2 == 0 else r - 1, c ^ 1))
    near = near_part(1, near, (both, *pieces[1:-1]), COST_B)
    both, pieces[0] = held([both, pieces[0]], [near])
    one, two = parted(both, arrived, rank)
    one = flipped(one, 2 ** (bits - 1), 0)
    near = near_part(2, near, (two,), COST_C)

    offsets = range(0, n_cols, 2)
    twos = [two] + [flipped(two, 0, offset) for offset in offsets[1:]]
    beside = flipped(two, 0, 1)
    one, pieces[-1], beside, *rest = held([one, pieces[-1], beside, *twos[1:]], [near])
    twos = [two] + rest
    ones = [
        one if (other, offset) == (0, 0) else flipped(one, other, offset)
        for other in range(2)
        for offset in offsets
    ]
    coeffs_two = [two, beside] + [x for there in rest for x in (there, flipped(there, 0, 1))]
    (halo,) = held([halo], coeffs_two[-1:])
    halos = (halo, flipped(halo, 0, 1))
    near = add_level(near, 1, left_two, pieces, coeffs_two, after=(halo,))
    ones = list(held(ones, [near]))
    coeffs_one = [x for there in ones for x in (there, flipped(there, 0, 1))]
    return near_field(*near_args, 0, 0, near, halos, (0, left_one, pieces, coeffs_one))


def solution(mesh):
    placed = (
        P("rows", None),
        P(("rows", "cols"), None, None, None),
        P(("rows", "cols"), None),
        P("rows", "cols"),
        P("rows", "cols"),
        P("rows", "cols"),
        P("rows", "cols"),
    )
    return jax.shard_map(
        per_device, mesh=mesh, in_specs=placed, out_specs=P(("rows", "cols"), None), check_vma=False
    )
```

```python
import jax
import jax.numpy as jnp
from jax import lax
from jax.experimental import pallas as pl
from jax.experimental.pallas import tpu as pltpu
from jax.sharding import PartitionSpec as P

B = 256
REACH = 2
AXES = ("rows", "cols")
VMEM = 64 * 1024 * 1024
COST_A = 1
COST_B = 1
COST_C = int(7000000000.0)
COST_D = int(10000000000.0)
HBM = pl.BlockSpec(memory_space=pltpu.HBM)
SMEM = pl.BlockSpec(memory_space=pltpu.SMEM)


def moved(value, target):
    n_rows, n_cols = lax.axis_size("rows"), lax.axis_size("cols")
    pairs = []
    for row in range(n_rows):
        for col in range(n_cols):
            other = target(row, col)
            if other is not None and 0 <= other[0] < n_rows:
                pairs.append((row * n_cols + col, other[0] * n_cols + other[1]))
    return lax.ppermute(value, AXES, pairs)


def flipped(value, row_bits, col_bits):
    return moved(value, lambda row, col: (row ^ row_bits, col ^ col_bits))


def span(index, size):
    return pl.ds(pl.multiple_of(index * size, size), size)


def called(kernel, name, smem, hbm, after, out_shape, scratch, aliases={}, flops=1):
    return pl.pallas_call(
        kernel,
        out_shape=out_shape,
        in_specs=[SMEM] * len(smem) + [HBM] * (len(hbm) + len(after)),
        out_specs=jax.tree.map(lambda _: HBM, out_shape),
        scratch_shapes=scratch,
        input_output_aliases=aliases,
        compiler_params=pltpu.CompilerParams(vmem_limit_bytes=VMEM),
        cost_estimate=pl.CostEstimate(flops=flops, bytes_accessed=1, transcendentals=0),
        name=name,
    )(*smem, *hbm, *after)


def project(right_one, right_two, vectors):
    depth, rank = right_one.shape
    width = vectors.shape[1]
    half = width // 2
    step = REACH * B
    parts = depth // step

    def kernel(one_ref, two_ref, vectors_ref, send_ref, keep_ref, *scratch):
        rights, block, total, result, right_sems, block_sems, out_sems = scratch
        mine = lax.axis_index("rows") % 2
        copies, places = [], []
        for i in range(parts):
            place = pl.ds(i * step, step)
            places.append(place)
            copies.append(
                [
                    pltpu.make_async_copy(
                        ref.at[place], rights.at[place, pl.ds(level * rank, rank)], right_sems.at[level, i]
                    )
                    for level, ref in enumerate((one_ref, two_ref))
                ]
                + [pltpu.make_async_copy(vectors_ref.at[place], block.at[place], block_sems.at[i])]
            )
            for copy in copies[-1]:
                copy.start()
        for i in range(parts):
            for copy in copies[i]:
                copy.wait()
            part = lax.dot_general(
                rights[places[i]], block[places[i]], (((0,), (0,)), ((), ())), preferred_element_type=jnp.float32
            )
            if i == 0:
                total[...] = part
            elif i < parts - 1:
                total[...] += part
            else:
                result[...] = (total[...] + part).astype(jnp.bfloat16)
        outs = []
        for k, (ref, chosen) in enumerate(((send_ref, mine ^ 1), (keep_ref, mine))):
            outs.append(
                pltpu.make_async_copy(
                    result.at[pl.ds(0, rank), span(chosen, half)], ref.at[pl.ds(0, rank)], out_sems.at[k, 0]
                )
            )
            for n in range(2):
                outs.append(
                    pltpu.make_async_copy(
                        result.at[pl.ds(rank, rank), pl.ds(n * half, half)],
                        ref.at[pl.ds((1 + n) * rank, rank)],
                        out_sems.at[k, 1 + n],
                    )
                )
        for copy in outs:
            copy.start()
        for copy in outs:
            copy.wait()

    return called(
        kernel,
        "project",
        [],
        [right_one, right_two, vectors],
        (),
        [
            jax.ShapeDtypeStruct((3 * rank, half), jnp.bfloat16),
            jax.ShapeDtypeStruct((3 * rank, half), jnp.bfloat16),
        ],
        [
            pltpu.VMEM((depth, 2 * rank), jnp.bfloat16),
            pltpu.VMEM((depth, width), jnp.bfloat16),
            pltpu.VMEM((2 * rank, width), jnp.float32),
            pltpu.VMEM((2 * rank, width), jnp.bfloat16),
            pltpu.SemaphoreType.DMA((2, parts)),
            pltpu.SemaphoreType.DMA((parts,)),
            pltpu.SemaphoreType.DMA((2, 3)),
        ],
    )


def near_field(near_cols, near_tiles, vectors, first, count, sofar=None, halos=(), sides=(0, 1), low_rank=None, after=(), flops=1):
    tiles, nnz = near_cols.shape
    rows, width = tiles * B, vectors.shape[1]
    half = width // 2
    window = vectors.shape[0] // B + 2 * REACH
    inside = count
    given = 0 if sofar is None else 1
    sizes = []
    while sum(sizes) < inside:
        sizes.append(min((1, 3, 4)[min(len(sizes), 2)], inside - sum(sizes)))
    if halos:
        sizes += [REACH] * len(halos)
    count = sum(sizes)
    near_groups = len(sizes)
    begins = [sum(sizes[:g]) * B for g in range(near_groups)] + [count * B]
    level, own, pieces, coeffs = low_rank or (0, None, (), ())
    rank = own.shape[1] if low_rank else 0
    offsets = len(pieces) + 1 if low_rank else 0
    whole = len(coeffs) == offsets
    depths = [size * B for size in sizes] + ([offsets * rank] if low_rank else [])
    groups, depth = len(depths), sum(depths)
    bound = [*halos, *([own, *pieces, *coeffs] if low_rank else [])]

    def kernel(cols_ref, tiles_ref, vectors_ref, *refs):
        sofar_refs, refs = refs[:given], refs[given:]
        halo_refs, refs = refs[: len(halos)], refs[len(halos) :]
        left_refs, refs = refs[:offsets], refs[offsets:]
        coeff_refs, refs = refs[: len(coeffs)], refs[len(coeffs) + len(after) :]
        out_ref, slots, wide, tall, total, result, *refs = refs
        tile_sems, tall_sems, rank_sems, sofar_sem, out_sems = refs
        mine, col = lax.axis_index("rows") % 2, lax.axis_index("cols")

        if count:
            for t in range(tiles):
                for c in range(window):
                    slots[t, c] = -1
                for k in range(nnz):
                    slots[t, cols_ref[t, k]] = k

        def tile_copy(t, c):
            if c < inside:
                place = first + c + REACH
            else:
                i = c - inside
                before = (sides[i // REACH] == 0) == (col % 2 == 1)
                place = jnp.where(before, i % REACH, window - REACH + i % REACH)
            slot = slots[t, place]
            copy = pltpu.make_async_copy(
                tiles_ref.at[t, jnp.maximum(slot, 0)],
                wide.at[pl.ds(t * B, B), pl.ds(c * B, B)],
                tile_sems.at[t, c],
            )
            return slot >= 0, copy

        def group_tiles(g):
            return [(t, c) for c in range(begins[g] // B, begins[g] // B + sizes[g]) for t in range(tiles)]

        def tall_copy(g):
            if begins[g] < inside * B:
                source = vectors_ref.at[pl.ds(first * B + begins[g], depths[g])]
            else:
                source = halo_refs[g - near_groups]
            return pltpu.make_async_copy(source, tall.at[pl.ds(begins[g], depths[g])], tall_sems.at[g])

        rank_copies = []
        for d in range(offsets):
            source = left_refs[d].at[level] if d else left_refs[0].at[span(col, rows)]
            place = pl.ds(count * B + d * rank, rank)
            rank_copies.append(pltpu.make_async_copy(source, wide.at[:, place], rank_sems.at[d, 2]))
            for n in range(2):
                if whole:
                    source, columns = coeff_refs[d].at[pl.ds(n * rank, rank)], pl.ds(n * half, half)
                else:
                    source, columns = coeff_refs[n * offsets + d], span(mine ^ n, half)
                rank_copies.append(pltpu.make_async_copy(source, tall.at[place, columns], rank_sems.at[d, n]))
        if given:
            sofar_copy = pltpu.make_async_copy(sofar_refs[0], result, sofar_sem)

        for g in range(near_groups):
            tall_copy(g).start()
            for t, c in group_tiles(g):
                there, copy = tile_copy(t, c)
                pl.when(there)(copy.start)

                @pl.when(jnp.logical_not(there))
                def _():
                    wide[t * B : (t + 1) * B, c * B : (c + 1) * B] = jnp.zeros((B, B), jnp.bfloat16)

        for copy in rank_copies:
            copy.start()
        if given:
            sofar_copy.start()
        outs = []
        for g in range(groups):
            last = g == groups - 1
            if g < near_groups:
                tall_copy(g).wait()
                for t, c in group_tiles(g):
                    there, copy = tile_copy(t, c)
                    pl.when(there)(copy.wait)
            else:
                for copy in rank_copies:
                    copy.wait()
            if last:
                if given:
                    sofar_copy.wait()
            chosen = pl.ds(begins[g], depths[g])
            cuts = 4 if last else 2
            for n in range(cuts):
                columns = pl.ds(n * (width // cuts), width // cuts)
                part = jnp.dot(wide[:, chosen], tall[chosen, columns], preferred_element_type=jnp.float32)
                if g > 0:
                    part = total[:, columns] + part
                if not last:
                    total[:, columns] = part
                else:
                    if given:
                        part = part + result[:, columns].astype(jnp.float32)
                    result[:, columns] = part.astype(jnp.bfloat16)
                    outs.append(
                        pltpu.make_async_copy(result.at[:, columns], out_ref.at[:, columns], out_sems.at[n])
                    )
                    outs[-1].start()
        for copy in outs:
            copy.wait()

    scratch = [
        pltpu.SMEM((tiles, window), jnp.int32),
        pltpu.VMEM((rows, depth), jnp.bfloat16),
        pltpu.VMEM((depth, width), jnp.bfloat16),
        pltpu.VMEM((rows, width), jnp.float32),
        pltpu.VMEM((rows, width), jnp.bfloat16),
        pltpu.SemaphoreType.DMA((tiles, max(count, 1))),
        pltpu.SemaphoreType.DMA((groups,)),
        pltpu.SemaphoreType.DMA((max(offsets, 1), 3)),
        pltpu.SemaphoreType.DMA,
        pltpu.SemaphoreType.DMA((4,)),
    ]
    return called(
        kernel,
        "near_field",
        [near_cols],
        [near_tiles, vectors] + ([sofar] if given else []) + bound,
        after,
        jax.ShapeDtypeStruct((rows, width), jnp.bfloat16),
        scratch,
        flops=flops,
    )


def packed(vectors, lefts, shares, after):
    depth, rank = lefts[0].shape
    rows = depth // shares

    edge, width = REACH * B, vectors.shape[1]

    def kernel(vectors_ref, one_ref, two_ref, *refs):
        refs = refs[len(after) :]
        edge_ref, out_refs, (rows_held, block, edge_sems, in_sems, out_sems) = refs[0], refs[1:shares], refs[shares:]
        col = lax.axis_index("cols")
        place = span(jnp.where(col % 2 == 0, depth // edge - 1, 0), edge)
        edge_in = pltpu.make_async_copy(vectors_ref.at[place], rows_held, edge_sems.at[0])
        edge_out = pltpu.make_async_copy(rows_held, edge_ref, edge_sems.at[1])
        ins = [
            [
                pltpu.make_async_copy(
                    ref.at[span(col ^ (d + 1), rows)], block.at[d, level], in_sems.at[d, level]
                )
                for level, ref in enumerate((one_ref, two_ref))
            ]
            for d in range(shares - 1)
        ]
        for copies in ins:
            for copy in copies:
                copy.start()
        edge_in.start()
        outs = []
        for d in range(shares - 1):
            for copy in ins[d]:
                copy.wait()
            outs.append(pltpu.make_async_copy(block.at[d], out_refs[d], out_sems.at[d]))
            outs[-1].start()
        edge_in.wait()
        edge_out.start()
        outs.append(edge_out)
        for copy in outs:
            copy.wait()

    return called(
        kernel,
        "packed",
        [],
        [vectors, *lefts],
        after,
        [jax.ShapeDtypeStruct((edge, width), jnp.bfloat16)]
        + [jax.ShapeDtypeStruct((2, rows, rank), jnp.bfloat16)] * (shares - 1),
        [
            pltpu.VMEM((edge, width), jnp.bfloat16),
            pltpu.VMEM((shares - 1, 2, rows, rank), jnp.bfloat16),
            pltpu.SemaphoreType.DMA((2,)),
            pltpu.SemaphoreType.DMA((shares - 1, 2)),
            pltpu.SemaphoreType.DMA((shares - 1,)),
        ],
    )


def parted(a, b, top):
    rows, width = b.shape

    def kernel(a_ref, b_ref, sum_ref, rest_ref, mine, theirs, total, sems):
        ins = [
            pltpu.make_async_copy(a_ref.at[pl.ds(0, top)], mine, sems.at[0]),
            pltpu.make_async_copy(b_ref.at[pl.ds(0, top)], theirs.at[pl.ds(0, top)], sems.at[1]),
            pltpu.make_async_copy(
                b_ref.at[pl.ds(top, rows - top)], theirs.at[pl.ds(top, rows - top)], sems.at[2]
            ),
        ]
        for copy in ins:
            copy.start()
        ins[0].wait()
        ins[1].wait()
        total[...] = (mine[...].astype(jnp.float32) + theirs[:top].astype(jnp.float32)).astype(jnp.bfloat16)
        outs = [
            pltpu.make_async_copy(total, sum_ref, sems.at[3]),
            pltpu.make_async_copy(theirs.at[pl.ds(top, rows - top)], rest_ref, sems.at[4]),
        ]
        outs[0].start()
        ins[2].wait()
        outs[1].start()
        for copy in outs:
            copy.wait()

    return called(
        kernel,
        "parted",
        [],
        [a, b],
        (),
        [
            jax.ShapeDtypeStruct((top, width), jnp.bfloat16),
            jax.ShapeDtypeStruct((rows - top, width), jnp.bfloat16),
        ],
        [
            pltpu.VMEM((top, width), jnp.bfloat16),
            pltpu.VMEM((rows, width), jnp.bfloat16),
            pltpu.VMEM((top, width), jnp.bfloat16),
            pltpu.SemaphoreType.DMA((5,)),
        ],
    )


def held(passed, after):
    def kernel(*refs):
        pass

    return called(
        kernel,
        "held",
        [],
        passed,
        after,
        [jax.ShapeDtypeStruct(x.shape, x.dtype) for x in passed],
        [],
        {i: i for i in range(len(passed))},
    )


def per_device(vectors, near_tiles, near_cols, left_one, right_one, left_two, right_two):
    n_rows, n_cols = lax.axis_size("rows"), lax.axis_size("cols")
    bits = n_rows.bit_length() - 1
    col = lax.axis_index("cols")
    depth = vectors.shape[0]
    rank = right_one.shape[1]
    inside = depth // B

    near_args = (near_cols, near_tiles, vectors)
    cuts = [0, inside // 4, 11 * inside // 16, inside]

    def near_part(part, sofar, after, flops):
        first, last = cuts[part : part + 2]
        return near_field(*near_args, first, last - first, sofar, after=after, flops=flops)

    def summed(a, b):
        return (a.astype(jnp.float32) + b.astype(jnp.float32)).astype(jnp.bfloat16)

    send, keep = project(right_one, right_two, vectors)
    arrived = flipped(send, 1, 0)

    edge, *pieces = packed(vectors, (left_one, left_two), n_cols, (keep,))
    pieces = [flipped(piece, 0, offset) for offset, piece in enumerate(pieces, 1)]

    near = near_part(0, None, (keep,), COST_A)
    (keep,) = held([keep], [near])
    both = summed(keep, arrived)
    for bit in range(1, bits - 2):
        both = summed(both, flipped(both, 2**bit, 0))
    arrived = flipped(both, 2 ** (bits - 2), 0)

    (edge,) = held([edge], [both])
    halo = moved(edge, lambda r, c: (r + 1 if c % 2 == 0 else r - 1, c ^ 1))
    near = near_part(1, near, (both, *pieces[1:-1]), COST_B)
    both, pieces[0] = held([both, pieces[0]], [near])
    one, two = parted(both, arrived, rank)
    one = flipped(one, 2 ** (bits - 1), 0)
    near = near_part(2, near, (two,), COST_C)

    offsets = range(0, n_cols, 2)
    twos = [two] + [flipped(two, 0, offset) for offset in offsets[1:]]
    beside = flipped(two, 0, 1)
    one, pieces[-1], beside, *rest = held([one, pieces[-1], beside, *twos[1:]], [near])
    twos = [two] + rest
    ones = [
        one if (other, offset) == (0, 0) else flipped(one, other, offset)
        for other in range(2)
        for offset in offsets
    ]
    coeffs_two = [two, beside] + [x for there in rest for x in (there, flipped(there, 0, 1))]
    (halo,) = held([halo], coeffs_two[-1:])
    halos = (halo, flipped(halo, 0, 1))
    near = near_field(
        *near_args, 0, 0, near, halos[:1], (0,), (1, left_two, pieces, coeffs_two), flops=COST_D
    )
    ones = list(held(ones, [near]))
    coeffs_one = [x for there in ones for x in (there, flipped(there, 0, 1))]
    return near_field(*near_args, 0, 0, near, halos[1:], (1,), (0, left_one, pieces, coeffs_one))


def solution(mesh):
    placed = (
        P("rows", None),
        P(("rows", "cols"), None, None, None),
        P(("rows", "cols"), None),
        P("rows", "cols"),
        P("rows", "cols"),
        P("rows", "cols"),
        P("rows", "cols"),
    )
    return jax.shard_map(
        per_device, mesh=mesh, in_specs=placed, out_specs=P(("rows", "cols"), None), check_vma=False
    )
```

```python
import jax
import jax.numpy as jnp
from jax import lax
from jax.experimental import pallas as pl
from jax.experimental.pallas import tpu as pltpu
from jax.sharding import PartitionSpec as P

B = 256
REACH = 2
AXES = ("rows", "cols")
VMEM = 64 * 1024 * 1024
COST_A = 1
COST_B = 1
COST_C = int(7000000000.0)
COST_D = int(10000000000.0)
HBM = pl.BlockSpec(memory_space=pltpu.HBM)
SMEM = pl.BlockSpec(memory_space=pltpu.SMEM)


def moved(value, target):
    n_rows, n_cols = lax.axis_size("rows"), lax.axis_size("cols")
    pairs = []
    for row in range(n_rows):
        for col in range(n_cols):
            other = target(row, col)
            if other is not None and 0 <= other[0] < n_rows:
                pairs.append((row * n_cols + col, other[0] * n_cols + other[1]))
    return lax.ppermute(value, AXES, pairs)


def flipped(value, row_bits, col_bits):
    return moved(value, lambda row, col: (row ^ row_bits, col ^ col_bits))


def span(index, size):
    return pl.ds(pl.multiple_of(index * size, size), size)


def called(kernel, name, smem, hbm, after, out_shape, scratch, aliases={}, flops=1):
    return pl.pallas_call(
        kernel,
        out_shape=out_shape,
        in_specs=[SMEM] * len(smem) + [HBM] * (len(hbm) + len(after)),
        out_specs=jax.tree.map(lambda _: HBM, out_shape),
        scratch_shapes=scratch,
        input_output_aliases=aliases,
        compiler_params=pltpu.CompilerParams(vmem_limit_bytes=VMEM),
        cost_estimate=pl.CostEstimate(flops=flops, bytes_accessed=1, transcendentals=0),
        name=name,
    )(*smem, *hbm, *after)


def project(right_one, right_two, vectors):
    depth, rank = right_one.shape
    width = vectors.shape[1]
    half = width // 2
    step = REACH * B
    parts = depth // step

    def kernel(one_ref, two_ref, vectors_ref, send_ref, keep_ref, *scratch):
        rights, block, total, result, right_sems, block_sems, out_sems = scratch
        mine = lax.axis_index("rows") % 2
        copies, places = [], []
        for i in range(parts):
            place = pl.ds(i * step, step)
            places.append(place)
            copies.append(
                [
                    pltpu.make_async_copy(
                        ref.at[place], rights.at[place, pl.ds(level * rank, rank)], right_sems.at[level, i]
                    )
                    for level, ref in enumerate((one_ref, two_ref))
                ]
                + [pltpu.make_async_copy(vectors_ref.at[place], block.at[place], block_sems.at[i])]
            )
            for copy in copies[-1]:
                copy.start()
        for i in range(parts):
            for copy in copies[i]:
                copy.wait()
            part = lax.dot_general(
                rights[places[i]], block[places[i]], (((0,), (0,)), ((), ())), preferred_element_type=jnp.float32
            )
            if i == 0:
                total[...] = part
            elif i < parts - 1:
                total[...] += part
            else:
                result[...] = (total[...] + part).astype(jnp.bfloat16)
        outs = []
        for k, (ref, chosen) in enumerate(((send_ref, mine ^ 1), (keep_ref, mine))):
            outs.append(
                pltpu.make_async_copy(
                    result.at[pl.ds(0, rank), span(chosen, half)], ref.at[pl.ds(0, rank)], out_sems.at[k, 0]
                )
            )
            for n in range(2):
                outs.append(
                    pltpu.make_async_copy(
                        result.at[pl.ds(rank, rank), pl.ds(n * half, half)],
                        ref.at[pl.ds((1 + n) * rank, rank)],
                        out_sems.at[k, 1 + n],
                    )
                )
        for copy in outs:
            copy.start()
        for copy in outs:
            copy.wait()

    return called(
        kernel,
        "project",
        [],
        [right_one, right_two, vectors],
        (),
        [
            jax.ShapeDtypeStruct((3 * rank, half), jnp.bfloat16),
            jax.ShapeDtypeStruct((3 * rank, half), jnp.bfloat16),
        ],
        [
            pltpu.VMEM((depth, 2 * rank), jnp.bfloat16),
            pltpu.VMEM((depth, width), jnp.bfloat16),
            pltpu.VMEM((2 * rank, width), jnp.float32),
            pltpu.VMEM((2 * rank, width), jnp.bfloat16),
            pltpu.SemaphoreType.DMA((2, parts)),
            pltpu.SemaphoreType.DMA((parts,)),
            pltpu.SemaphoreType.DMA((2, 3)),
        ],
    )


def near_field(near_cols, near_tiles, vectors, first, count, sofar=None, halos=(), sides=(0, 1), low_rank=None, after=(), flops=1):
    tiles, nnz = near_cols.shape
    rows, width = tiles * B, vectors.shape[1]
    half = width // 2
    window = vectors.shape[0] // B + 2 * REACH
    inside = count
    given = 0 if sofar is None else 1
    sizes = []
    while sum(sizes) < inside:
        sizes.append(min((1, 3, 4)[min(len(sizes), 2)], inside - sum(sizes)))
    if halos:
        sizes += [REACH] * len(halos)
    count = sum(sizes)
    near_groups = len(sizes)
    begins = [sum(sizes[:g]) * B for g in range(near_groups)] + [count * B]
    level, own, pieces, coeffs = low_rank or (0, None, (), ())
    rank = own.shape[1] if low_rank else 0
    offsets = len(pieces) + 1 if low_rank else 0
    whole = len(coeffs) == offsets
    depths = [size * B for size in sizes] + ([offsets * rank] if low_rank else [])
    groups, depth = len(depths), sum(depths)
    bound = [*halos, *([own, *pieces, *coeffs] if low_rank else [])]

    def kernel(cols_ref, tiles_ref, vectors_ref, *refs):
        sofar_refs, refs = refs[:given], refs[given:]
        halo_refs, refs = refs[: len(halos)], refs[len(halos) :]
        left_refs, refs = refs[:offsets], refs[offsets:]
        coeff_refs, refs = refs[: len(coeffs)], refs[len(coeffs) + len(after) :]
        out_ref, slots, wide, tall, total, result, *refs = refs
        tile_sems, tall_sems, rank_sems, sofar_sem, out_sems = refs
        mine, col = lax.axis_index("rows") % 2, lax.axis_index("cols")

        if count:
            for t in range(tiles):
                for c in range(window):
                    slots[t, c] = -1
                for k in range(nnz):
                    slots[t, cols_ref[t, k]] = k

        def tile_copy(t, c):
            if c < inside:
                place = first + c + REACH
            else:
                i = c - inside
                before = (sides[i // REACH] == 0) == (col % 2 == 1)
                place = jnp.where(before, i % REACH, window - REACH + i % REACH)
            slot = slots[t, place]
            copy = pltpu.make_async_copy(
                tiles_ref.at[t, jnp.maximum(slot, 0)],
                wide.at[pl.ds(t * B, B), pl.ds(c * B, B)],
                tile_sems.at[t, c],
            )
            return slot >= 0, copy

        def group_tiles(g):
            return [(t, c) for c in range(begins[g] // B, begins[g] // B + sizes[g]) for t in range(tiles)]

        def tall_copy(g):
            if begins[g] < inside * B:
                source = vectors_ref.at[pl.ds(first * B + begins[g], depths[g])]
            else:
                source = halo_refs[g - near_groups]
            return pltpu.make_async_copy(source, tall.at[pl.ds(begins[g], depths[g])], tall_sems.at[g])

        rank_copies = []
        for d in range(offsets):
            source = left_refs[d].at[level] if d else left_refs[0].at[span(col, rows)]
            place = pl.ds(count * B + d * rank, rank)
            rank_copies.append(pltpu.make_async_copy(source, wide.at[:, place], rank_sems.at[d, 2]))
            for n in range(2):
                if whole:
                    source, columns = coeff_refs[d].at[pl.ds(n * rank, rank)], pl.ds(n * half, half)
                else:
                    source, columns = coeff_refs[n * offsets + d], span(mine ^ n, half)
                rank_copies.append(pltpu.make_async_copy(source, tall.at[place, columns], rank_sems.at[d, n]))
        if given:
            sofar_copy = pltpu.make_async_copy(sofar_refs[0], result, sofar_sem)

        for g in range(near_groups):
            tall_copy(g).start()
            for t, c in group_tiles(g):
                there, copy = tile_copy(t, c)
                pl.when(there)(copy.start)

                @pl.when(jnp.logical_not(there))
                def _():
                    wide[t * B : (t + 1) * B, c * B : (c + 1) * B] = jnp.zeros((B, B), jnp.bfloat16)

        for copy in rank_copies:
            copy.start()
        if given:
            sofar_copy.start()
        outs = []
        for g in range(groups):
            last = g == groups - 1
            if g < near_groups:
                tall_copy(g).wait()
                for t, c in group_tiles(g):
                    there, copy = tile_copy(t, c)
                    pl.when(there)(copy.wait)
            else:
                for copy in rank_copies:
                    copy.wait()
            if last:
                if given:
                    sofar_copy.wait()
            chosen = pl.ds(begins[g], depths[g])
            cuts = 4 if last else 2
            for n in range(cuts):
                columns = pl.ds(n * (width // cuts), width // cuts)
                part = jnp.dot(wide[:, chosen], tall[chosen, columns], preferred_element_type=jnp.float32)
                if g > 0:
                    part = total[:, columns] + part
                if not last:
                    total[:, columns] = part
                else:
                    if given:
                        part = part + result[:, columns].astype(jnp.float32)
                    result[:, columns] = part.astype(jnp.bfloat16)
                    outs.append(
                        pltpu.make_async_copy(result.at[:, columns], out_ref.at[:, columns], out_sems.at[n])
                    )
                    outs[-1].start()
        for copy in outs:
            copy.wait()

    scratch = [
        pltpu.SMEM((tiles, window), jnp.int32),
        pltpu.VMEM((rows, depth), jnp.bfloat16),
        pltpu.VMEM((depth, width), jnp.bfloat16),
        pltpu.VMEM((rows, width), jnp.float32),
        pltpu.VMEM((rows, width), jnp.bfloat16),
        pltpu.SemaphoreType.DMA((tiles, max(count, 1))),
        pltpu.SemaphoreType.DMA((groups,)),
        pltpu.SemaphoreType.DMA((max(offsets, 1), 3)),
        pltpu.SemaphoreType.DMA,
        pltpu.SemaphoreType.DMA((4,)),
    ]
    return called(
        kernel,
        "near_field",
        [near_cols],
        [near_tiles, vectors] + ([sofar] if given else []) + bound,
        after,
        jax.ShapeDtypeStruct((rows, width), jnp.bfloat16),
        scratch,
        flops=flops,
    )


def packed(vectors, lefts, shares, after):
    depth, rank = lefts[0].shape
    rows = depth // shares

    edge, width = REACH * B, vectors.shape[1]

    def kernel(vectors_ref, one_ref, two_ref, *refs):
        refs = refs[len(after) :]
        edge_ref, out_refs, (rows_held, block, edge_sems, in_sems, out_sems) = refs[0], refs[1:shares], refs[shares:]
        col = lax.axis_index("cols")
        place = span(jnp.where(col % 2 == 0, depth // edge - 1, 0), edge)
        edge_in = pltpu.make_async_copy(vectors_ref.at[place], rows_held, edge_sems.at[0])
        edge_out = pltpu.make_async_copy(rows_held, edge_ref, edge_sems.at[1])
        ins = [
            [
                pltpu.make_async_copy(
                    ref.at[span(col ^ (d + 1), rows)], block.at[d, level], in_sems.at[d, level]
                )
                for level, ref in enumerate((one_ref, two_ref))
            ]
            for d in range(shares - 1)
        ]
        for copies in ins:
            for copy in copies:
                copy.start()
        edge_in.start()
        outs = []
        for d in range(shares - 1):
            for copy in ins[d]:
                copy.wait()
            outs.append(pltpu.make_async_copy(block.at[d], out_refs[d], out_sems.at[d]))
            outs[-1].start()
        edge_in.wait()
        edge_out.start()
        outs.append(edge_out)
        for copy in outs:
            copy.wait()

    return called(
        kernel,
        "packed",
        [],
        [vectors, *lefts],
        after,
        [jax.ShapeDtypeStruct((edge, width), jnp.bfloat16)]
        + [jax.ShapeDtypeStruct((2, rows, rank), jnp.bfloat16)] * (shares - 1),
        [
            pltpu.VMEM((edge, width), jnp.bfloat16),
            pltpu.VMEM((shares - 1, 2, rows, rank), jnp.bfloat16),
            pltpu.SemaphoreType.DMA((2,)),
            pltpu.SemaphoreType.DMA((shares - 1, 2)),
            pltpu.SemaphoreType.DMA((shares - 1,)),
        ],
    )


def parted(a, b, top):
    rows, width = b.shape

    def kernel(a_ref, b_ref, sum_ref, rest_ref, mine, theirs, total, sems):
        ins = [
            pltpu.make_async_copy(a_ref.at[pl.ds(0, top)], mine, sems.at[0]),
            pltpu.make_async_copy(b_ref.at[pl.ds(0, top)], theirs.at[pl.ds(0, top)], sems.at[1]),
            pltpu.make_async_copy(
                b_ref.at[pl.ds(top, rows - top)], theirs.at[pl.ds(top, rows - top)], sems.at[2]
            ),
        ]
        for copy in ins:
            copy.start()
        ins[0].wait()
        ins[1].wait()
        total[...] = (mine[...].astype(jnp.float32) + theirs[:top].astype(jnp.float32)).astype(jnp.bfloat16)
        outs = [
            pltpu.make_async_copy(total, sum_ref, sems.at[3]),
            pltpu.make_async_copy(theirs.at[pl.ds(top, rows - top)], rest_ref, sems.at[4]),
        ]
        outs[0].start()
        ins[2].wait()
        outs[1].start()
        for copy in outs:
            copy.wait()

    return called(
        kernel,
        "parted",
        [],
        [a, b],
        (),
        [
            jax.ShapeDtypeStruct((top, width), jnp.bfloat16),
            jax.ShapeDtypeStruct((rows - top, width), jnp.bfloat16),
        ],
        [
            pltpu.VMEM((top, width), jnp.bfloat16),
            pltpu.VMEM((rows, width), jnp.bfloat16),
            pltpu.VMEM((top, width), jnp.bfloat16),
            pltpu.SemaphoreType.DMA((5,)),
        ],
    )


def held(passed, after):
    def kernel(*refs):
        pass

    return called(
        kernel,
        "held",
        [],
        passed,
        after,
        [jax.ShapeDtypeStruct(x.shape, x.dtype) for x in passed],
        [],
        {i: i for i in range(len(passed))},
    )


def per_device(vectors, near_tiles, near_cols, left_one, right_one, left_two, right_two):
    n_rows, n_cols = lax.axis_size("rows"), lax.axis_size("cols")
    bits = n_rows.bit_length() - 1
    col = lax.axis_index("cols")
    depth = vectors.shape[0]
    rank = right_one.shape[1]
    inside = depth // B

    near_args = (near_cols, near_tiles, vectors)
    cuts = [0, inside // 4, 5 * inside // 8, inside]

    def near_part(part, sofar, after, flops):
        first, last = cuts[part : part + 2]
        return near_field(*near_args, first, last - first, sofar, after=after, flops=flops)

    def summed(a, b):
        return (a.astype(jnp.float32) + b.astype(jnp.float32)).astype(jnp.bfloat16)

    send, keep = project(right_one, right_two, vectors)
    arrived = flipped(send, 1, 0)

    edge, *pieces = packed(vectors, (left_one, left_two), n_cols, (keep,))
    pieces = [flipped(piece, 0, offset) for offset, piece in enumerate(pieces, 1)]

    near = near_part(0, None, (keep,), COST_A)
    (keep,) = held([keep], [near])
    both = summed(keep, arrived)
    for bit in range(1, bits - 2):
        both = summed(both, flipped(both, 2**bit, 0))
    arrived = flipped(both, 2 ** (bits - 2), 0)

    (edge,) = held([edge], [both])
    halo = moved(edge, lambda r, c: (r + 1 if c % 2 == 0 else r - 1, c ^ 1))
    near = near_part(1, near, (both, *pieces[1:-1]), COST_B)
    both, pieces[0] = held([both, pieces[0]], [near])
    one, two = parted(both, arrived, rank)
    one = flipped(one, 2 ** (bits - 1), 0)
    near = near_part(2, near, (two,), COST_C)

    offsets = range(0, n_cols, 2)
    twos = [two] + [flipped(two, 0, offset) for offset in offsets[1:]]
    beside = flipped(two, 0, 1)
    one, pieces[-1], beside, *rest = held([one, pieces[-1], beside, *twos[1:]], [near])
    twos = [two] + rest
    ones = [
        one if (other, offset) == (0, 0) else flipped(one, other, offset)
        for other in range(2)
        for offset in offsets
    ]
    coeffs_two = [two, beside] + [x for there in rest for x in (there, flipped(there, 0, 1))]
    (halo,) = held([halo], coeffs_two[-1:])
    halos = (halo, flipped(halo, 0, 1))
    near = near_field(
        *near_args, 0, 0, near, halos[:1], (0,), (1, left_two, pieces, coeffs_two), flops=COST_D
    )
    ones = list(held(ones, [near]))
    coeffs_one = [x for there in ones for x in (there, flipped(there, 0, 1))]
    return near_field(*near_args, 0, 0, near, halos[1:], (1,), (0, left_one, pieces, coeffs_one))


def solution(mesh):
    placed = (
        P("rows", None),
        P(("rows", "cols"), None, None, None),
        P(("rows", "cols"), None),
        P("rows", "cols"),
        P("rows", "cols"),
        P("rows", "cols"),
        P("rows", "cols"),
    )
    return jax.shard_map(
        per_device, mesh=mesh, in_specs=placed, out_specs=P(("rows", "cols"), None), check_vma=False
    )
```
